256 devices in a mesh: cls: 4 (over y), ptcl: 64 (over x, z, core).
Axes of the slice: x: 4, y: 4, z: 8, core: 2. Of those that a mesh axis runs over, the one named last changes fastest.
Arguments:
- images: bfloat16 [8192, 8192], P('ptcl'), may hold values from -0.125 to 0.125
- bin_lists: int32 [8192, 2], P('ptcl'), may hold values from 0 to 63, all different within a row; in each aligned block of 128 rows (0 to 127, 128 to 255, ...) at most 8 rows name the same one
- precision: bfloat16 [8192], P('ptcl'), may hold values from 0.35 to 2048
- references: bfloat16 [4, 32768, 8192], P('cls', 'ptcl'), may hold values from -1.5 to 1.5
- line_index: int32 [4, 32768, 64], P('cls', 'ptcl'), may hold values from 0 to 127
- interp_blocks: bfloat16 [64, 128, 128], replicated, may hold values from -0.5 to 0.5
Outputs:
- class_prob: float32 [8192, 4], P('ptcl', 'cls')
- volume: float32 [4, 8192, 128], P('cls', 'ptcl')
The draws below stay inside these ranges and needn't reach their ends.
Inputs may be any that keep to these rules, and one draw needn't show every extreme that they name: `bin_lists`: each particle names 2 different bins; among the particles of one index of ptcl no bin is named more than 8 times, and in some draws' devices some bin exactly 8 times.
All inputs are finite; a program needn't handle non-finite values.
Results may differ from the reference program's by a relative error of at most 0.0034.
Values may be sent and summed in bfloat16 or wider, within the bound.
A program may use at most 128 MiB of HBM per device.

```python
import math
import jax
import jax.numpy as jnp
import numpy as np
from jax import lax

LINE = 128
LINES = 64
PIX = 8192
P_DEV = 128
PARTICLES = 8192
TOPB = 2
CAP = 8
REF_DEV = 512
REFS = 32768
CLS = 4
VLINES = 8192
N_PTCL = 64


def draw_precision(key, part):
    key = jax.random.fold_in(key, 5)
    base_key = jax.random.fold_in(key, 0)
    uniform_draw = jax.random.uniform(base_key, (PARTICLES,), jnp.float32)
    values = jnp.exp(jnp.log(0.35) + uniform_draw * (jnp.log(1.0) - jnp.log(0.35)))
    return values.astype(jnp.bfloat16)


def draw_references(key, part):
    key = jax.random.fold_in(key, 17)
    mode_key, scale_key, value_key = jax.random.split(key, 3)
    upper_mode = jax.random.randint(mode_key, (CLS, REFS, 1), 0, 2) == 1
    scale_draw = jax.random.uniform(scale_key, (CLS, REFS, 1), jnp.float32)
    low_scale = jnp.exp(jnp.log(0.6) + scale_draw * (jnp.log(0.85) - jnp.log(0.6)))
    high_scale = jnp.exp(jnp.log(2.55) + scale_draw * (jnp.log(2.7) - jnp.log(2.55)))
    row_scale = jnp.where(upper_mode, high_scale, low_scale)
    values = jax.random.truncated_normal(value_key, -4.0, 4.0, (CLS, REFS, PIX), jnp.float32)
    return (values * row_scale * PIX ** (-0.5)).astype(jnp.bfloat16)


def with_ends(array, stream_key, smallest, high):
    longest = array.shape.index(max(array.shape))
    spots = []
    for shift in (0, 1):
        where = [jax.random.randint(jax.random.fold_in(stream_key, axis), (), 0, length) for axis, length in enumerate(array.shape)]
        where[longest] = (where[longest] + shift) % array.shape[longest]
        spots.append(tuple(where))
    return array.at[spots[0]].set(smallest).at[spots[1]].set(high)


def shard_levels(own_key, extent, shards, least, high):
    def one(dim, blocks):
        draws = jax.random.uniform(jax.random.fold_in(jax.random.fold_in(own_key, 6), dim), (blocks,), jnp.float32, least / len(shards), high / len(shards))
        return jnp.repeat(jnp.exp(draws), extent[dim] // blocks).reshape((-1,) + (1,) * (len(extent) - dim - 1))

    gain = one(*shards[0])
    for cut in shards[1:]:
        gain = gain * one(*cut)
    return gain


def deal_out(rng, own, number, rows, count, top, limit, slope):
    ranking = jax.random.permutation(rng, count)
    crowded, usual = portions_of(count, rows * top, limit, slope, True), portions_of(count, rows * top, limit, slope, False)
    places = jnp.arange(count)

    def named(tallies, turn):
        used = int((tallies > 0).sum())
        fixed = max(1, used // 4)
        passed = fixed + (places - fixed + turn * (used - fixed)) % max(1, count - fixed)
        return jnp.zeros((count,), jnp.int32).at[ranking[jnp.where(places < fixed, places, passed)]].set(jnp.asarray(tallies, jnp.int32))

    tallies = jnp.where(number % 4 == 0, named(crowded, number // 4), named(usual, number - number // 4 - 1))
    mixed = jax.random.permutation(jax.random.fold_in(own, 3), count)
    source_of, receiver = mixed[0:count // 2 * 2:2], mixed[1:count // 2 * 2:2]
    margin = jnp.minimum(tallies[source_of] - 1, limit - tallies[receiver]) // 2
    margin = jnp.where((source_of == ranking[0]) | (receiver == ranking[0]) | (tallies[receiver] == 0), 0, jnp.maximum(margin, 0))
    passed = jax.random.randint(jax.random.fold_in(own, 4), (count // 2,), 0, 1 << 20) % (margin + 1)
    tallies = tallies.at[source_of].add(-passed).at[receiver].add(passed)
    members = jnp.searchsorted(jnp.cumsum(tallies), jnp.arange(rows * top), side="right").astype(jnp.int32)
    listing = members.reshape(top, rows).T
    listing = listing[jax.random.permutation(jax.random.fold_in(own, 1), rows)]
    turn = jax.random.randint(jax.random.fold_in(own, 2), (rows, 1), 0, top)
    return jnp.take_along_axis(listing, (jnp.arange(top)[None, :] + turn) % top, axis=1)


def portions_of(number_of, total, reach, skew, full):
    loads = [(1 << 20) // math.isqrt(grade ** skew) + 1 for grade in range(1, number_of + 1)]
    largest = reach if full else min(reach, max(-(-total // number_of), total * loads[0] // sum(loads)))
    least = 1 if total - largest >= number_of - 1 else 0
    counts, surplus = [largest] + [least] * (number_of - 1), total - largest - least * (number_of - 1)
    while surplus > 0:
        free = [i for i in range(1, number_of) if counts[i] < largest] or [i for i in range(1, number_of) if counts[i] < reach]
        mass, remaining = sum([loads[i] for i in free]), surplus
        for i in free:
            more = min(reach - counts[i], max(1, remaining * loads[i] // mass), surplus)
            counts[i] = counts[i] + more
            surplus = surplus - more
    return np.array(counts)


def normal_values(stream_key, dims, deviation, most, shards=(), kind=jnp.bfloat16):
    gain = shard_levels(stream_key, dims, shards, -0.22, 0.18) if shards else 1.0
    array = jax.random.normal(stream_key, dims, jnp.float32) * deviation * gain
    return jnp.minimum(jnp.maximum(array, -most), most).astype(kind)


def setup_inputs(seed: int = 0) -> dict:
    splits = jax.random.split(jax.random.key(seed), 7)
    images = normal_values(splits[0], (PARTICLES, PIX), 0.02, 0.125, ((0, 64),))
    bin_lists_keys = jax.random.split(jax.random.fold_in(splits[1], 1), PARTICLES // P_DEV)
    bin_lists_turns = jax.random.permutation(jax.random.fold_in(splits[1], 3), PARTICLES // P_DEV)
    bin_lists = jax.vmap(lambda own, number: deal_out(jax.random.fold_in(splits[1], 2), own, number, P_DEV, N_PTCL, TOPB, CAP, 2))(bin_lists_keys, bin_lists_turns).reshape((PARTICLES, TOPB))
    precision = draw_precision(jax.random.fold_in(splits[6], 71), 0)
    references = draw_references(jax.random.fold_in(splits[6], 71), 0)
    line_index = with_ends(jax.random.randint(splits[4], (CLS, REFS, LINES), 0, VLINES // LINES), jax.random.fold_in(splits[4], 1), 0, (VLINES // LINES) - 1).astype(jnp.int32)
    interp_blocks = normal_values(splits[5], (LINES, LINE, LINE), LINE ** -0.5, 0.5)
    return {"images": images, "bin_lists": bin_lists, "precision": precision, "references": references, "line_index": line_index, "interp_blocks": interp_blocks}


def slot_layout(bin_rows, peers, spaces):
    flat_bins = bin_rows.reshape(-1).astype(jnp.int32)
    onehot = (flat_bins[:, None] == jnp.arange(peers, dtype=jnp.int32)[None, :]).astype(jnp.int32)
    position = jnp.sum((jnp.cumsum(onehot, axis=0) - onehot) * onehot, axis=1).astype(jnp.int32)
    slot_id = (flat_bins * spaces + position).astype(jnp.int32)
    source = (jnp.arange(flat_bins.shape[0], dtype=jnp.int32) // bin_rows.shape[1]).astype(jnp.int32)
    filled = jnp.zeros((peers * spaces,), jnp.int32).at[slot_id].set(1)
    slot_src = jnp.zeros((peers * spaces,), jnp.int32).at[slot_id].set(source)
    return filled, slot_src


def reference(images, bin_lists, precision, references, line_index, interp_blocks):
    def layout_one(bin_rows):
        return slot_layout(bin_rows, N_PTCL, CAP)

    filled, slot_src = jax.vmap(layout_one)(bin_lists.reshape(N_PTCL, P_DEV, TOPB))
    offsets = (jnp.arange(N_PTCL, dtype=jnp.int32) * P_DEV)[:, None]
    global_idx = (slot_src + offsets).astype(jnp.int32)
    global_idx = global_idx.reshape(N_PTCL, N_PTCL, CAP).transpose(1, 0, 2).reshape(N_PTCL, N_PTCL * CAP)
    filled_dst = filled.reshape(N_PTCL, N_PTCL, CAP).transpose(1, 0, 2).reshape(N_PTCL, N_PTCL * CAP)
    slot_scale = precision.astype(jnp.float32)[global_idx] * filled_dst.astype(jnp.float32)
    ref_rows = references.reshape(CLS, N_PTCL, REF_DEV, PIX)

    def class_scores(refs_class):
        def bin_scores(entries):
            refs_bin, idx_bin, scale_bin = entries
            pixel_rows = images[idx_bin]
            products = lax.dot_general(pixel_rows, refs_bin, (((1,), (1,)), ((), ())),
                                       preferred_element_type=jnp.float32)
            half_norm = 0.5 * jnp.sum(jnp.square(refs_bin.astype(jnp.float32)), axis=1)
            return scale_bin[:, None] * (products - half_norm[None, :])
        return lax.map(bin_scores, (refs_class, global_idx, slot_scale))

    scores = lax.map(class_scores, ref_rows)
    highest = jnp.max(scores, axis=3)
    totals = jnp.sum(jnp.exp(scores - highest[..., None]), axis=3)
    occupied = jnp.broadcast_to(filled_dst > 0, highest.shape)
    owners_full = jnp.broadcast_to(global_idx, highest.shape)
    owners = owners_full.reshape(-1)
    masked_top = jnp.where(occupied, highest, -jnp.inf)
    maximum = jax.ops.segment_max(masked_top.reshape(-1), owners, num_segments=PARTICLES)
    part_mass = jnp.where(occupied, totals * jnp.exp(highest - maximum[owners_full]), 0.0)
    log_total = maximum + jnp.log(jax.ops.segment_sum(part_mass.reshape(-1), owners, num_segments=PARTICLES))
    relative = jnp.where(occupied, totals * jnp.exp(highest - log_total[owners_full]), 0.0)

    def class_sum(relative_class):
        return jax.ops.segment_sum(relative_class.reshape(-1), global_idx.reshape(-1), num_segments=PARTICLES)

    class_prob = jax.vmap(class_sum)(relative).T
    slot_log = jnp.where(filled_dst > 0, log_total[global_idx], 1e30)
    band_start = (jnp.arange(LINES, dtype=jnp.int32) * (VLINES // LINES))[None, None, :]
    placed = (line_index + band_start).astype(jnp.int32)
    index_rows = placed.reshape(CLS, N_PTCL, REF_DEV * LINES)
    blocks_wide = interp_blocks.astype(jnp.float32)

    def class_volume(entries):
        scores_class, index_class = entries

        def add_bin(volume, entries_bin):
            score_bin, idx_bin, log_bin, place_bin = entries_bin
            weights = (REF_DEV * jnp.exp(score_bin - log_bin[:, None])).astype(jnp.bfloat16)
            pixel_rows = images[idx_bin]
            class_image = lax.dot_general(weights, pixel_rows, (((0,), (0,)), ((), ())),
                                          preferred_element_type=jnp.float32).astype(jnp.bfloat16)
            line_part = jnp.einsum("rlk,lkj->rlj", class_image.reshape(REF_DEV, LINES, LINE).astype(jnp.float32),
                                   blocks_wide, precision=lax.Precision.HIGHEST)
            return volume.at[place_bin].add(line_part.reshape(-1, LINE)), None

        volume, unused = lax.scan(add_bin, jnp.zeros((VLINES, LINE), jnp.float32),
                                  (scores_class, global_idx, slot_log, index_class))
        return volume

    volume = lax.map(class_volume, (scores, index_rows))
    return class_prob, volume
```

```python
import functools

import jax
import jax.numpy as jnp
from jax import lax
from jax.experimental import pallas as pl
from jax.experimental.pallas import tpu as pltpu
from jax.sharding import PartitionSpec as P

MESH = pl.DeviceIdType.MESH
F32, BF16, I32 = jnp.float32, jnp.bfloat16, jnp.int32
NZ = 8
CW = 256
LINE = 128
SLOTS = 8


def iota(shape, dim):
    return lax.broadcasted_iota(I32, shape, dim)


def dot(a, b, ca=1, cb=0):
    return lax.dot_general(a, b, (((ca,), (cb,)), ((), ())), preferred_element_type=F32)


def thirds(v):
    hi = v.astype(BF16)
    rest = v - hi.astype(F32)
    mid = rest.astype(BF16)
    low = (rest - mid.astype(F32)).astype(BF16)
    return hi, mid, low


def kernel(ny, nx, nz, nch, img_hbm, meta_ref, refs_hbm, idx_ref, interp_hbm, prob_ref, vol_ref,
           img, meta, g, g2, sendbuf, recv, xs_all, refs, onehot, interp, score, weight, hnorm,
           psend, ptab, stat, bsend, btab, csend, ctab, vb, sib, xs, xr, zs, zr,
           load_sem, ex_ss, ex_rs, a_ss, a_rs, a_loc, p_ss, p_rs, k_ss, k_rs, k_loc,
           y_ss, y_rs, f_ss, f_rs, s_ss, s_rs, b_ss, b_rs, c_ss, c_rs,
           v_ss, v_rs, x_ss, x_rs, z_ss, z_rs):
    nq = nx * nz
    y, d = lax.axis_index("cls"), lax.axis_index("ptcl")
    q, k = d // 2, d % 2
    x, z = q // nz, q % nz
    other = 1 - k
    part = meta_ref.shape[1]
    span = nch * CW
    n_ref = refs.shape[0]
    rows = nq * 16
    nw = rows // 128
    sibling = (y, q * 2 + other)
    y_up, y_dn = (y + 1) % ny, (y + ny - 1) % ny
    up, dn = (y_up, d), (y_dn, d)

    def remote(src, dst, ss, rs, dev):
        return pltpu.make_async_remote_copy(src_ref=src, dst_ref=dst, send_sem=ss, recv_sem=rs,
                                            device_id=dev, device_id_type=MESH)

    ld_img = pltpu.make_async_copy(
        img_hbm.at[:, pl.ds(pl.multiple_of((y * 2 + k) * span, span), span)], img.at[k], load_sem.at[0])
    ld_refs = pltpu.make_async_copy(refs_hbm, refs, load_sem.at[1])
    ld_int = pltpu.make_async_copy(interp_hbm, interp, load_sem.at[2])
    ld_img.start()
    ld_refs.start()
    ld_int.start()

    bar = pltpu.get_barrier_semaphore()

    def greet(i, c):
        q2 = (q + i) % nq
        pl.semaphore_signal(bar, inc=1, device_id=(y, q2 * 2 + k), device_id_type=MESH)
        return c

    lax.fori_loop(1, nq, greet, 0)

    def greet_col(i, c):
        c2 = (y * 2 + k + i) % (2 * ny)
        pl.semaphore_signal(bar, inc=1, device_id=(c2 // 2, q * 2 + c2 % 2), device_id_type=MESH)
        return c

    lax.fori_loop(1, 2 * ny, greet_col, 0)
    pl.semaphore_wait(bar, nq - 1 + 2 * ny - 1)

    ex_meta = remote(meta_ref, meta.at[k], ex_ss.at[0], ex_rs.at[0], sibling)
    ex_meta.start()
    ex_img = remote(img_hbm.at[:, pl.ds(pl.multiple_of((y * 2 + other) * span, span), span)], img.at[k],
                    ex_ss.at[1], ex_rs.at[1], sibling)
    ex_img.start()
    meta[k] = meta_ref[...]
    ex_meta.wait_recv()

    both = meta[...]
    n_bin, pairs = nq * 2, 2 * part
    before = (iota((pairs, pairs), 0) < iota((pairs, pairs), 1)).astype(F32).astype(BF16)
    r = iota((2 * rows, n_bin), 0)
    row_bin = (lax.shift_right_logical(r, 4) % nq) * 2 + lax.shift_right_logical(r, 4) // nq
    expand = (row_bin == iota((2 * rows, n_bin), 1)).astype(F32).astype(BF16)
    r2 = iota((2 * rows, pairs), 0)
    folded = []
    for k2 in range(2):
        bins = jnp.concatenate([both[k2, 0:1], both[k2, 1:2]], axis=1)
        named = (iota((n_bin, pairs), 0).astype(F32) == bins).astype(F32)
        rank = dot(named.astype(BF16), before)
        marked = (named * (rank + 1.0)).astype(BF16)
        spread = dot(expand, marked)
        want = jnp.where((lax.shift_right_logical(r2, 3) & 1) == k2, (r2 & 7) + 1, -1).astype(F32)
        hit = (spread == want).astype(F32)
        g2[:, :, k2 * pairs:(k2 + 1) * pairs] = hit.astype(BF16).reshape(2, rows, pairs)
        folded.append(hit[:, :part] + hit[:, part:])
    g[...] = jnp.concatenate(folded, axis=1).astype(BF16)

    ld_img.wait()
    ex_img.wait_recv()
    for j in range(nch):
        cols = slice(j * CW, (j + 1) * CW)
        pix = jnp.concatenate([img[0, :, cols], img[1, :, cols]], axis=0)
        sendbuf[j] = dot(g[...], pix).astype(BF16).reshape(2, nq, 16, CW)

        def send(i, c):
            q2 = (q + i) % nq
            remote(sendbuf.at[j, :, q2], recv.at[j, :, q], a_ss.at[j], a_rs.at[j], (y, q2 * 2 + k)).start()
            return c

        lax.fori_loop(1, nq, send, 0)
        pltpu.make_async_copy(sendbuf.at[j, :, q], recv.at[j, :, q], a_loc.at[j]).start()

    def scatter(src, dst, ss, rs):
        def one(i, c):
            q2 = (q + i) % nq
            remote(src.at[q2 // 8], dst.at[q], ss, rs, (y, q2 * 2 + k)).start()
            return c

        lax.fori_loop(1, nq, one, 0)
        dst[q] = src[q // 8]

    def gathered(dst, ss, rs):
        remote(dst.at[pl.ds(0, nq - 1)], dst.at[pl.ds(0, nq - 1)], ss, rs, sibling).wait_recv()

    def sent(dst, ss, rs):
        remote(dst.at[pl.ds(0, nq - 1)], dst.at[pl.ds(0, nq - 1)], ss, rs, sibling).wait_send()

    def windows(dst, value):
        for w in range(nw):
            dst[w] = value[:, w * 128:(w + 1) * 128]

    def unpack(tab):
        t = tab[...]
        lane = iota(t.shape, 2)
        t = jnp.where(lax.shift_right_logical(lane, 4) == q % 8, t, 0.0)
        t = t.reshape(nq * 8, 128)
        for s in (64, 32, 16):
            t = t + pltpu.roll(t, s, 1)
        t = jnp.concatenate([t] * nw, axis=1).reshape(nq, 8, rows)
        keep = lax.shift_right_logical(iota(t.shape, 2), 4) == iota(t.shape, 0)
        return jnp.sum(jnp.where(keep, t, 0.0), axis=0)

    prec = jnp.concatenate([both[0, 2:3], both[0, 2:3], both[1, 2:3], both[1, 2:3]], axis=1)
    prec = jnp.broadcast_to(prec, (8, 2 * pairs)).astype(BF16)
    windows(psend, dot(prec, g2[k], 1, 1))
    scatter(psend, ptab, p_ss, p_rs)

    ld_refs.wait()
    hnorm[...] = jnp.zeros_like(hnorm)

    def norm(i, c):
        v = refs[:, pl.ds(pl.multiple_of(i * 128, 128), 128)].astype(F32)
        hnorm[...] += v * v
        return c

    lax.fori_loop(0, refs.shape[1] // 128, norm, 0)
    half = 0.5 * jnp.sum(hnorm[...], axis=1, keepdims=True)

    def bands(i, c):
        onehot[i] = (iota((LINE, n_ref), 0) == idx_ref[pl.ds(i, 1), :]).astype(F32).astype(BF16)
        return c

    lax.fori_loop(0, onehot.shape[0], bands, 0)
    score[...] = jnp.zeros_like(score)

    def piece(yy, k2, j):
        return (yy * 2 + k2) * nch + j

    def add_score(p):
        r_p = refs[:, pl.ds(pl.multiple_of(p * CW, CW), CW)]
        score[...] += dot(r_p, xs_all[p].reshape(rows, CW), 1, 1)

    def y_copy(src, p, way, k2, j):
        return remote(src, xs_all.at[p], y_ss.at[way, k2, j], y_rs.at[way, k2, j], up if way == 0 else dn)

    def y_wait(yy, way, k2, j):
        p = piece(yy, k2, j)
        remote(xs_all.at[p], xs_all.at[p], y_ss.at[way, k2, j], y_rs.at[way, k2, j], up).wait_recv()

    def f_copy(p, way, j):
        return remote(xs_all.at[p], xs_all.at[p], f_ss.at[way, j], f_rs.at[way, j], up if way == 0 else dn)

    def chunk_wait(j):
        remote(recv.at[j, :, pl.ds(0, nq - 1)], recv.at[j, :, pl.ds(0, nq - 1)], a_ss.at[j], a_rs.at[j],
               sibling).wait_recv()
        pltpu.make_async_copy(sendbuf.at[j, :, q], recv.at[j, :, q], a_loc.at[j]).wait()

    def own_copy(j):
        return pltpu.make_async_copy(recv.at[j, k], xs_all.at[piece(y, k, j)], k_loc.at[j])

    def sib_copy(j):
        return remote(recv.at[j, other], xs_all.at[piece(y, k, j)], k_ss.at[j], k_rs.at[j], sibling)

    def stage0(j):
        chunk_wait(j)
        sib_copy(j).start()
        for way in range(2):
            y_copy(recv.at[j, k], piece(y, k, j), way, k, j).start()
        own_copy(j).start()
        sib_copy(j).wait_recv()
        for way in range(2):
            y_copy(xs_all.at[piece(y, other, j)], piece(y, other, j), way, other, j).start()
        own_copy(j).wait()

    def stage1(j):
        y_wait(y_dn, 0, 0, j)
        f_copy(piece(y_dn, 0, j), 0, j).start()
        y_wait(y_up, 1, 1, j)
        f_copy(piece(y_up, 1, j), 1, j).start()
        add_score(piece(y, 0, j))
        add_score(piece(y, 1, j))
        add_score(piece(y_dn, 0, j))
        add_score(piece(y_up, 1, j))
        y_wait(y_dn, 0, 1, j)
        y_wait(y_up, 1, 0, j)
        add_score(piece(y_dn, 1, j))
        add_score(piece(y_up, 0, j))

    def stage2(j):
        far = (y + 2) % ny
        for way in range(2):
            f_copy(piece(far, way, j), way, j).wait_recv()
            add_score(piece(far, way, j))

    for j in range(nch + 2):
        if j < nch:
            stage0(j)
        if 1 <= j <= nch:
            stage1(j - 1)
        if j >= 2:
            stage2(j - 2)

    gathered(ptab, p_ss, p_rs)
    scale = unpack(ptab)[0:1]
    s = scale * (score[...] - half)
    score[...] = s
    top = jnp.max(s, axis=0, keepdims=True)
    total = jnp.sum(jnp.exp(s - top), axis=0, keepdims=True)
    col = y * 2 + k
    stat[col] = jnp.concatenate([top, total], axis=0)

    def share(i, c):
        c2 = (col + i) % (2 * ny)
        remote(stat.at[col], stat.at[col], s_ss, s_rs, (c2 // 2, q * 2 + c2 % 2)).start()
        return c

    lax.fori_loop(1, 2 * ny, share, 0)
    all_stat = stat.at[pl.ds(0, 2 * ny - 1)]
    remote(all_stat, all_stat, s_ss, s_rs, sibling).wait_recv()
    line = [[], [], []]
    for kb in range(2):
        tops = [stat[2 * yy + kb, 0:1] for yy in range(ny)]
        high = functools.reduce(jnp.maximum, tops)
        mass = sum(stat[2 * yy + kb, 1:2] * jnp.exp(tops[yy] - high) for yy in range(ny))
        mine = stat[2 * y + kb]
        line[0].append(high)
        line[1].append(mass)
        line[2].append(mine[1:2] * jnp.exp(mine[0:1] - high))
    table = jnp.concatenate(line[0] + line[1] + line[2] + [jnp.zeros((2, rows), F32)], axis=0)
    windows(bsend, table)
    scatter(bsend, btab, b_ss, b_rs)

    gathered(btab, b_ss, b_rs)
    cut = jnp.concatenate(thirds(unpack(btab)), axis=0)
    per_pair = []
    for kb in range(2):
        t = dot(cut, g2[kb])
        per_pair.append((t[16:24] + t[8:16]) + t[0:8])
    highs = per_pair[0][0:1] + per_pair[1][1:2]
    masses = per_pair[0][2:3] + per_pair[1][3:4]
    own = per_pair[0][4:5] + per_pair[1][5:6]
    logs, probs = [], []
    for k2 in range(2):
        lo, mi, hi = k2 * pairs, k2 * pairs + part, (k2 + 1) * pairs
        m0, m1 = highs[:, lo:mi], highs[:, mi:hi]
        high = jnp.maximum(m0, m1)
        log = high + jnp.log(masses[:, lo:mi] * jnp.exp(m0 - high) + masses[:, mi:hi] * jnp.exp(m1 - high))
        probs.append(own[:, lo:mi] * jnp.exp(m0 - log) + own[:, mi:hi] * jnp.exp(m1 - log))
        logs += [log, log]
    prob_ref[...] = jnp.where(k == 0, probs[0], probs[1])
    cut = jnp.concatenate(thirds(jnp.concatenate(logs, axis=1)) + (jnp.zeros((5, 2 * pairs), BF16),), axis=0)
    t = dot(cut, g2[k], 1, 1)
    slot_log = (t[2:3] + t[1:2]) + t[0:1]
    windows(csend, jnp.broadcast_to(slot_log, (8, rows)))
    scatter(csend, ctab, c_ss, c_rs)
    gathered(ctab, c_ss, c_rs)
    slot_log = unpack(ctab)[0:1]
    weight[...] = (n_ref * jnp.exp(score[...] - slot_log)).astype(BF16)

    ld_int.wait()

    def sib_send(t):
        return remote(vb.at[t, :, other], sib.at[t], v_ss.at[t], v_rs.at[t], sibling)

    def x_send(t, i):
        x2 = (x + nx - 1 - i) % nx
        return remote(xs.at[t, i], xr.at[t, i], x_ss.at[t], x_rs.at[t], (y, (x2 * nz + z) * 2 + k))

    def x_all(t):
        ref = xr.at[t]
        return remote(ref, ref, x_ss.at[t], x_rs.at[t], sibling)

    def z_send(t):
        z2 = (z + nz - 1 - t) % nz
        return remote(zs.at[t], zr.at[t], z_ss.at[t], z_rs.at[t], (y, (x * nz + z2) * 2 + k))

    def insert(t, i):
        q2 = ((x + nx - 1 - i) % nx) * nz + (z + nz - 1 - t) % nz
        image = dot(weight[...], xs_all[q2].reshape(rows, CW)).astype(BF16)
        for h in range(2):
            band = dot(onehot[2 * q2 + h], image[:, h * LINE:(h + 1) * LINE])
            hi = band.astype(BF16)
            low = (band - hi.astype(F32)).astype(BF16)
            block = interp[2 * q2 + h]
            vb[t, i, h] = dot(jnp.concatenate([hi, low], axis=1), jnp.concatenate([block, block], axis=0))

    def step(t, c):
        @pl.when(t < nz)
        def _():
            lax.fori_loop(0, nx, lambda i, c: (insert(t, i), c)[1], 0)
            sib_send(t).start()

        @pl.when((t >= 1) & (t <= nz))
        def _():
            u = t - 1
            sib_send(u).wait_recv()

            def one(i, c):
                xs[u, i] = (vb[u, i, k] + sib[u, i]).astype(BF16)
                x_send(u, i).start()
                return c

            lax.fori_loop(0, nx - 1, one, 0)

        @pl.when(t >= 2)
        def _():
            u = t - 2
            x_all(u).wait_recv()
            total = vb[u, nx - 1, k] + sib[u, nx - 1]
            for i in range(nx - 1):
                total += xr[u, i].astype(F32)

            @pl.when(u < nz - 1)
            def _():
                zs[u] = total.astype(BF16)
                z_send(u).start()

            @pl.when(u == nz - 1)
            def _():
                vol_ref[...] = total

        return c

    lax.fori_loop(0, nz + 2, step, 0)

    def z_add(t, c):
        z_send(t).wait_recv()
        vol_ref[...] += zr[t].astype(F32)
        return c

    lax.fori_loop(0, nz - 1, z_add, 0)

    ex_meta.wait_send()
    ex_img.wait_send()
    sent(ptab, p_ss, p_rs)
    remote(all_stat, all_stat, s_ss, s_rs, sibling).wait_send()
    sent(btab, b_ss, b_rs)
    sent(ctab, c_ss, c_rs)
    for j in range(nch):
        ref = recv.at[j, :, pl.ds(0, nq - 1)]
        remote(ref, ref, a_ss.at[j], a_rs.at[j], sibling).wait_send()
        sib_copy(j).wait_send()
        for way in range(2):
            y_copy(recv.at[j, k], piece(y, k, j), way, k, j).wait_send()
            y_copy(xs_all.at[piece(y, other, j)], piece(y, other, j), way, other, j).wait_send()
        f_copy(piece(y_dn, 0, j), 0, j).wait_send()
        f_copy(piece(y_up, 1, j), 1, j).wait_send()

    def v_done(t, c):
        sib_send(t).wait_send()
        x_all(t).wait_send()
        return c

    lax.fori_loop(0, nz, v_done, 0)
    lax.fori_loop(0, nz - 1, lambda t, c: (z_send(t).wait_send(), c)[1], 0)


def local(nz, images, bin_lists, precision, references, line_index, interp_blocks):
    ny, n_ptcl = lax.axis_size("cls"), lax.axis_size("ptcl")
    nq = n_ptcl // 2
    nx = nq // nz
    part, pixels = images.shape
    n_ref = references.shape[1]
    n_line = interp_blocks.shape[0]
    nch = pixels // (2 * ny * CW)
    rows = nq * 16
    nw = rows // 128
    meta = jnp.concatenate([bin_lists.T.astype(F32), precision.astype(F32)[None], jnp.zeros((5, part), F32)], axis=0)
    vmem, dma = pltpu.VMEM, pltpu.SemaphoreType.DMA
    whole = pl.BlockSpec(memory_space=pltpu.VMEM)
    far = pl.BlockSpec(memory_space=pl.ANY)
    flops = 4 * n_ref * rows * pixels
    prob, volume = pl.pallas_call(
        functools.partial(kernel, ny, nx, nz, nch),
        out_shape=(jax.ShapeDtypeStruct((1, part), F32), jax.ShapeDtypeStruct((LINE, LINE), F32)),
        in_specs=[far, whole, far, whole, far],
        out_specs=(whole, whole),
        scratch_shapes=[
            vmem((2, part, nch * CW), BF16),
            vmem((2, 8, part), F32),
            vmem((2 * rows, 2 * part), BF16),
            vmem((2, rows, 4 * part), BF16),
            vmem((nch, 2, nq, 16, CW), BF16),
            vmem((nch, 2, nq, 16, CW), BF16),
            vmem((2 * ny * nch, nq, 16, CW), BF16),
            vmem((n_ref, pixels), BF16),
            vmem((n_line, LINE, n_ref), BF16),
            vmem((n_line, LINE, LINE), BF16),
            vmem((n_ref, rows), F32),
            vmem((n_ref, rows), BF16),
            vmem((n_ref, 128), F32),
            vmem((nw, 8, 128), F32), vmem((nq, 8, 128), F32),
            vmem((2 * ny, 2, rows), F32),
            vmem((nw, 8, 128), F32), vmem((nq, 8, 128), F32),
            vmem((nw, 8, 128), F32), vmem((nq, 8, 128), F32),
            vmem((nz, nx, 2, LINE, LINE), F32),
            vmem((nz, nx, LINE, LINE), F32),
            vmem((nz, nx - 1, LINE, LINE), BF16), vmem((nz, nx - 1, LINE, LINE), BF16),
            vmem((nz - 1, LINE, LINE), BF16), vmem((nz - 1, LINE, LINE), BF16),
            dma((3,)), dma((2,)), dma((2,)),
            dma((nch,)), dma((nch,)), dma((nch,)),
            dma(()), dma(()),
            dma((nch,)), dma((nch,)), dma((nch,)),
            dma((2, 2, nch)), dma((2, 2, nch)),
            dma((2, nch)), dma((2, nch)),
            dma(()), dma(()), dma(()), dma(()), dma(()), dma(()),
            dma((nz,)), dma((nz,)), dma((nz,)), dma((nz,)), dma((nz - 1,)), dma((nz - 1,)),
        ],
        compiler_params=pltpu.CompilerParams(collective_id=0, has_side_effects=True, vmem_limit_bytes=58 << 20),
        cost_estimate=pl.CostEstimate(flops=flops, bytes_accessed=n_ref * pixels * 2, transcendentals=0),
    )(images, meta, references[0], line_index[0].T, interp_blocks)
    return prob.reshape(part, 1), volume[None]


def solution(mesh, nz=NZ):
    in_specs = (
        P("ptcl", None),
        P("ptcl", None),
        P("ptcl"),
        P("cls", "ptcl", None),
        P("cls", "ptcl", None),
        P(),
    )
    out_specs = (P("ptcl", "cls"), P("cls", "ptcl", None))
    return jax.shard_map(functools.partial(local, nz), mesh=mesh, in_specs=in_specs, out_specs=out_specs,
                         check_vma=False)
```

```python
import functools

import jax
import jax.numpy as jnp
from jax import lax
from jax.experimental import pallas as pl
from jax.experimental.pallas import tpu as pltpu
from jax.sharding import PartitionSpec as P

MESH = pl.DeviceIdType.MESH
F32, BF16, I32 = jnp.float32, jnp.bfloat16, jnp.int32
NZ = 8
CW = 128
FAR = 2
LINE = 128
SLOTS = 8


def iota(shape, dim):
    return lax.broadcasted_iota(I32, shape, dim)


def dot(a, b, ca=1, cb=0):
    return lax.dot_general(a, b, (((ca,), (cb,)), ((), ())), preferred_element_type=F32)


def thirds(v):
    hi = v.astype(BF16)
    rest = v - hi.astype(F32)
    mid = rest.astype(BF16)
    low = (rest - mid.astype(F32)).astype(BF16)
    return hi, mid, low


def kernel(ny, nx, nz, nch, far_n, img_hbm, bins_ref, prec_ref, refs_hbm, idx_ref, interp_hbm, prob_ref, vol_ref,
           img, meta, g, g2, sendbuf, recv, xs_all, refs, onehot, interp, score, weight, hnorm,
           psend, ptab, stat, lrow, ltab, dsend, dtab, vb, sib, xs, xr, zs, zr,
           load_sem, ex_ss, ex_rs, a_ss, a_rs, a_loc, p_ss, p_rs, k_ss, k_rs, k_loc,
           y_ss, y_rs, f_ss, f_rs, s_ss, s_rs, b_ss, b_rs, d_ss, d_rs,
           v_ss, v_rs, x_ss, x_rs, z_ss, z_rs):
    nq = nx * nz
    y, d = lax.axis_index("cls"), lax.axis_index("ptcl")
    q, k = d // 2, d % 2
    x, z = q // nz, q % nz
    other = 1 - k
    part = bins_ref.shape[1]
    n_bin, pairs = nq * 2, 2 * part
    n_chunk = nch + far_n
    n_ref = refs.shape[0]
    rows = nq * 16
    nw = rows // 128
    sibling = (y, q * 2 + other)
    y_up, y_dn, y_far = (y + 1) % ny, (y + ny - 1) % ny, (y + 2) % ny
    up, dn = (y_up, d), (y_dn, d)

    def remote(src, dst, ss, rs, dev):
        return pltpu.make_async_remote_copy(src_ref=src, dst_ref=dst, send_sem=ss, recv_sem=rs,
                                            device_id=dev, device_id_type=MESH)

    def piece(yy, k2, j):
        return (yy * 2 + k2) * nch + j

    def pixels(p, count):
        return pl.ds(pl.multiple_of(p * CW, CW), count * CW)

    def plane(i):
        return (y, ((q + i) % nq) * 2 + k)

    bar = pltpu.get_barrier_semaphore()

    def greet(i, c):
        pl.semaphore_signal(bar, inc=1, device_id=(y, (d + i) % n_bin), device_id_type=MESH)
        return c

    def greet_y(i, c):
        pl.semaphore_signal(bar, inc=1, device_id=((y + i) % ny, d), device_id_type=MESH)
        return c

    lax.fori_loop(1, n_bin, greet, 0)
    lax.fori_loop(1, ny, greet_y, 0)

    def img_parts(core):
        return ((img_hbm.at[:, pixels(piece(y, core, 0), nch)], img.at[k, :, pl.ds(0, nch * CW)]),
                (img_hbm.at[:, pixels(piece(y_far, core, nch - far_n), far_n)],
                 img.at[k, :, pl.ds(nch * CW, far_n * CW)]))

    ld_img = [pltpu.make_async_copy(a, b, load_sem.at[i]) for i, (a, b) in enumerate(img_parts(k))]
    ld_refs = pltpu.make_async_copy(refs_hbm, refs, load_sem.at[2])
    ld_int = pltpu.make_async_copy(interp_hbm, interp, load_sem.at[3])
    for ld in ld_img + [ld_refs, ld_int]:
        ld.start()
    meta[k, 0:2] = bins_ref[...].astype(F32)
    meta[k, 2:3] = prec_ref[...].astype(F32)
    meta[k, 3:8] = jnp.zeros((5, part), F32)
    before = (iota((pairs, pairs), 0) < iota((pairs, pairs), 1)).astype(F32).astype(BF16)
    r = iota((2 * rows, n_bin), 0)
    row_bin = (lax.shift_right_logical(r, 4) % nq) * 2 + lax.shift_right_logical(r, 4) // nq
    expand = (row_bin == iota((2 * rows, n_bin), 1)).astype(F32).astype(BF16)
    pl.semaphore_wait(bar, n_bin - 1 + ny - 1)

    ex = [remote(meta.at[k], meta.at[k], ex_ss.at[0], ex_rs.at[0], sibling)]
    ex += [remote(a, b, ex_ss.at[1 + i], ex_rs.at[1 + i], sibling) for i, (a, b) in enumerate(img_parts(other))]
    for e in ex:
        e.start()
    ex[0].wait_recv()

    both = meta[...]
    r2 = iota((2 * rows, pairs), 0)
    folded, mates, mate_ranks, precs = [], [], [], []
    for k2 in range(2):
        bins = jnp.concatenate([both[k2, 0:1], both[k2, 1:2]], axis=1)
        named = (iota((n_bin, pairs), 0).astype(F32) == bins).astype(F32)
        rank = named * dot(named.astype(BF16), before)
        spread = dot(expand, (named + rank).astype(BF16))
        want = jnp.where((lax.shift_right_logical(r2, 3) & 1) == k2, (r2 & 7) + 1, -1).astype(F32)
        hit = (spread == want).astype(F32)
        g2[:, :, k2 * pairs:(k2 + 1) * pairs] = hit.astype(BF16).reshape(2, rows, pairs)
        folded.append(hit[:, :part] + hit[:, part:])
        ranks = jnp.sum(rank, axis=0, keepdims=True)
        mates += [both[k2, 1:2], both[k2, 0:1]]
        mate_ranks += [ranks[:, part:], ranks[:, :part]]
        precs += [both[k2, 2:3]] * 2
    g[...] = jnp.concatenate(folded, axis=1).astype(BF16)

    def send_chunks(j, n):
        cols = slice(j * CW, (j + n) * CW)
        pix = jnp.concatenate([img[0, :, cols], img[1, :, cols]], axis=0)
        out = dot(g[...], pix).astype(BF16)
        for m in range(n):
            sendbuf[j + m] = out[:, m * CW:(m + 1) * CW].reshape(2, nq, 16, CW)

            def send(i, c):
                remote(sendbuf.at[j + m, :, (q + i) % nq], recv.at[j + m, :, q], a_ss.at[j + m], a_rs.at[j + m],
                       plane(i)).start()
                return c

            lax.fori_loop(1, nq, send, 0)
            pltpu.make_async_copy(sendbuf.at[j + m, :, q], recv.at[j + m, :, q], a_loc.at[j + m]).start()

    ld_img[0].wait()
    ex[1].wait_recv()
    for j in range(0, nch, 2):
        send_chunks(j, min(2, nch - j))
    ld_img[1].wait()
    ex[2].wait_recv()
    for j in range(nch, n_chunk, 2):
        send_chunks(j, min(2, n_chunk - j))

    def windows(dst, value):
        for w in range(nw):
            dst[w] = value[:, w * 128:(w + 1) * 128]

    def own_lanes(t):
        axis = t.ndim - 1
        t = jnp.where(lax.shift_right_logical(iota(t.shape, axis), 4) == q % 8, t, 0.0)
        for s in (64, 32, 16):
            t = t + pltpu.roll(t, s, axis)
        return t

    def by_chip(t):
        n = t.shape[1]
        t = t.reshape(nw, 8, n, 128)
        t = jnp.sum(jnp.where(lax.shift_right_logical(iota(t.shape, 3), 4) == iota(t.shape, 1), t, 0.0), axis=1)
        return jnp.concatenate([t[w] for w in range(nw)], axis=1)

    facts = [jnp.concatenate(v, axis=1) for v in (precs, mates, mate_ranks)]
    facts = jnp.concatenate(facts + [jnp.zeros((5, 2 * pairs), F32)], axis=0).astype(BF16)
    windows(psend, dot(facts, g2[k], 1, 1))

    def send_facts(i, c):
        remote(psend.at[((q + i) % nq) // 8], ptab.at[q], p_ss, p_rs, plane(i)).start()
        return c

    lax.fori_loop(1, nq, send_facts, 0)
    ptab[q] = psend[q // 8]
    facts_done = remote(ptab.at[pl.ds(0, nq - 1)], ptab.at[pl.ds(0, nq - 1)], p_ss, p_rs, sibling)

    ld_refs.wait()
    hnorm[...] = jnp.zeros_like(hnorm)

    def norm(i, c):
        v = refs[:, pl.ds(pl.multiple_of(i * 128, 128), 128)].astype(F32)
        hnorm[...] += v * v
        return c

    lax.fori_loop(0, refs.shape[1] // 128, norm, 0)

    def bands(i, c):
        onehot[i] = (iota((LINE, n_ref), 0) == idx_ref[pl.ds(i, 1), :]).astype(F32).astype(BF16)
        return c

    lax.fori_loop(0, onehot.shape[0], bands, 0)
    score[...] = jnp.zeros_like(score)

    def slab(p):
        return jnp.concatenate([xs_all[p].reshape(rows, CW), xs_all[p + 1].reshape(rows, CW)], axis=1)

    def add_score(p):
        score[...] += dot(refs[:, pixels(p, 2)], slab(p), 1, 1)

    def y_copy(src, p, way, k2, j):
        return remote(src, xs_all.at[p], y_ss.at[way, k2, j], y_rs.at[way, k2, j], up if way == 0 else dn)

    def y_wait(yy, way, k2, j):
        p = piece(yy, k2, j)
        remote(xs_all.at[p], xs_all.at[p], y_ss.at[way, k2, j], y_rs.at[way, k2, j], up).wait_recv()

    def f_copy(p, way, j):
        return remote(xs_all.at[p], xs_all.at[p], f_ss.at[way, j], f_rs.at[way, j], up if way == 0 else dn)

    def chunk_wait(j):
        ref = recv.at[j, :, pl.ds(0, nq - 1)]
        remote(ref, ref, a_ss.at[j], a_rs.at[j], sibling).wait_recv()
        pltpu.make_async_copy(sendbuf.at[j, :, q], recv.at[j, :, q], a_loc.at[j]).wait()

    def home(k2, j):
        return piece(y, k2, j) if j < nch else piece(y_far, k2, j - far_n)

    def own_copy(j):
        return pltpu.make_async_copy(recv.at[j, k], xs_all.at[home(k, j)], k_loc.at[j])

    def sib_copy(j):
        return remote(recv.at[j, other], xs_all.at[home(k, j)], k_ss.at[j], k_rs.at[j], sibling)

    def stage0(j):
        chunk_wait(j)
        sib_copy(j).start()
        own_copy(j).start()
        if j < nch:
            for way in range(2):
                y_copy(recv.at[j, k], piece(y, k, j), way, k, j).start()
        sib_copy(j).wait_recv()
        if j < nch:
            for way in range(2):
                y_copy(xs_all.at[piece(y, other, j)], piece(y, other, j), way, other, j).start()
        own_copy(j).wait()

    def stage1(j):
        y_wait(y_dn, 0, 0, j)
        if j < nch - far_n:
            f_copy(piece(y_dn, 0, j), 0, j).start()
        y_wait(y_up, 1, 1, j)
        if j < nch - far_n:
            f_copy(piece(y_up, 1, j), 1, j).start()
        if j % 2:
            for k2 in range(2):
                add_score(piece(y, k2, j - 1))
            add_score(piece(y_dn, 0, j - 1))
            add_score(piece(y_up, 1, j - 1))
        y_wait(y_dn, 0, 1, j)
        y_wait(y_up, 1, 0, j)
        if j % 2:
            add_score(piece(y_dn, 1, j - 1))
            add_score(piece(y_up, 0, j - 1))

    def stage2(j):
        if j < nch - far_n:
            for way in range(2):
                f_copy(piece(y_far, way, j), way, j).wait_recv()
        if j % 2:
            for way in range(2):
                add_score(piece(y_far, way, j - 1))

    for j in range(nch):
        stage0(j)
        if j >= 1:
            stage1(j - 1)
        if 2 <= j and j - 2 < nch - far_n - far_n % 2:
            stage2(j - 2)
    stage1(nch - 1)
    for j in range(nch, n_chunk):
        stage0(j)
    for j in range(nch - 2 if nch - 2 < nch - far_n - far_n % 2 else nch - far_n - far_n % 2, nch):
        stage2(j)

    facts_done.wait_recv()
    known = by_chip(own_lanes(ptab[...]))
    half = 0.5 * jnp.sum(hnorm[...], axis=1, keepdims=True)
    s = known[0:1] * (score[...] - half)
    score[...] = s
    top = jnp.max(s, axis=0, keepdims=True)
    total = jnp.sum(jnp.exp(s - top), axis=0, keepdims=True)
    stat[y] = jnp.concatenate([top, total], axis=0)

    def share(i, c):
        remote(stat.at[y], stat.at[y], s_ss, s_rs, ((y + i) % ny, d)).start()
        return c

    lax.fori_loop(1, ny, share, 0)
    mate = known[1:2] * 8.0 + known[2:3]
    mate = jnp.concatenate([mate[:, w * 128:(w + 1) * 128] for w in range(nw)], axis=0)
    all_stat = stat.at[pl.ds(0, ny - 1)]
    remote(all_stat, all_stat, s_ss, s_rs, sibling).wait_recv()
    tops = [stat[yy, 0:1] for yy in range(ny)]
    high = functools.reduce(jnp.maximum, tops)
    mine = high + jnp.log(sum(stat[yy, 1:2] * jnp.exp(tops[yy] - high) for yy in range(ny)))
    mine = jnp.concatenate([mine[:, w * 128:(w + 1) * 128] for w in range(nw)], axis=0)

    lrow[...] = mine

    def spread_sums(i, c):
        remote(lrow, ltab.at[d], b_ss, b_rs, (y, (d + i) % n_bin)).start()
        return c

    lax.fori_loop(1, n_bin, spread_sums, 0)
    ltab[d] = mine
    all_sums = ltab.at[pl.ds(0, n_bin - 1)]
    remote(all_sums, all_sums, b_ss, b_rs, sibling).wait_recv()
    sums = ltab[...]
    slot = iota((nw, 128), 1) & 7
    key = iota(sums.shape, 0) * 8 + (iota(sums.shape, 2) & 7)
    key = key.astype(F32)
    theirs = jnp.zeros((nw, 128), F32)
    for delta in range(1 - SLOTS, SLOTS):
        asked = pltpu.roll(mate, delta % 128, 1)
        asked = jnp.where((slot - delta >= 0) & (slot - delta < SLOTS), asked, -1.0)
        found = jnp.sum(jnp.where(key == asked[None], sums, 0.0), axis=0)
        theirs = theirs + pltpu.roll(found, (-delta) % 128, 1)
    high = jnp.maximum(mine, theirs)
    log = high + jnp.log(jnp.exp(mine - high) + jnp.exp(theirs - high))
    log = jnp.concatenate([log[w:w + 1] for w in range(nw)], axis=1)
    weight[...] = (n_ref * jnp.exp(score[...] - log)).astype(BF16)

    windows(dsend, stat[y][1:2] * jnp.exp(stat[y][0:1] - log))

    def send_prob(i, c):
        d2 = (d + i) % n_bin
        remote(dsend.at[d2 // 16], dtab.at[d], d_ss, d_rs, (y, d2)).start()
        return c

    lax.fori_loop(1, n_bin, send_prob, 0)
    dtab[d] = dsend[d // 16]
    prob_done = remote(dtab.at[pl.ds(0, n_bin - 1)], dtab.at[pl.ds(0, n_bin - 1)], d_ss, d_rs, sibling)

    ld_int.wait()

    def sib_send(t):
        return remote(vb.at[t, :, other], sib.at[t], v_ss.at[t], v_rs.at[t], sibling)

    def x_send(t, i):
        x2 = (x + nx - 1 - i) % nx
        return remote(xs.at[t, i], xr.at[t, i], x_ss.at[t], x_rs.at[t], (y, (x2 * nz + z) * 2 + k))

    def x_all(t):
        ref = xr.at[t]
        return remote(ref, ref, x_ss.at[t], x_rs.at[t], sibling)

    def z_send(t):
        z2 = (z + nz - 1 - t) % nz
        return remote(zs.at[t], zr.at[t], z_ss.at[t], z_rs.at[t], (y, (x * nz + z2) * 2 + k))

    def insert(t):
        chips = [((x + nx - 1 - i) % nx) * nz + (z + nz - 1 - t) % nz for i in range(nx)]
        images = [dot(weight[...], slab(2 * c)).astype(BF16) for c in chips]
        sums = [dot(onehot[2 * c + h], im[:, h * LINE:(h + 1) * LINE]) for c, im in zip(chips, images) for h in (0, 1)]
        out = []
        for i in range(nx):
            for h in range(2):
                band = sums[2 * i + h]
                hi = band.astype(BF16)
                low = (band - hi.astype(F32)).astype(BF16)
                block = interp[2 * chips[i] + h]
                out.append(dot(jnp.concatenate([hi, low], axis=1), jnp.concatenate([block, block], axis=0)))
        for i in range(nx):
            for h in range(2):
                vb[t, i, h] = out[2 * i + h]

    def step(t, c):
        @pl.when(t < nz)
        def _():
            insert(t)
            sib_send(t).start()

        @pl.when((t >= 1) & (t <= nz))
        def _():
            u = t - 1
            sib_send(u).wait_recv()

            def one(i, c):
                xs[u, i] = (vb[u, i, k] + sib[u, i]).astype(BF16)
                x_send(u, i).start()
                return c

            lax.fori_loop(0, nx - 1, one, 0)

        @pl.when(t >= 2)
        def _():
            u = t - 2
            x_all(u).wait_recv()
            total = vb[u, nx - 1, k] + sib[u, nx - 1]
            for i in range(nx - 1):
                total += xr[u, i].astype(F32)

            @pl.when(u < nz - 1)
            def _():
                zs[u] = total.astype(BF16)
                z_send(u).start()

            @pl.when(u == nz - 1)
            def _():
                vol_ref[...] = total

        return c

    lax.fori_loop(0, nz + 2, step, 0)

    prob_done.wait_recv()
    t = own_lanes(dtab[...]).reshape(nq, 2, 128)
    t = by_chip(t)
    found = jnp.zeros((8, 2 * pairs), F32)
    for kb in range(2):
        cut = jnp.concatenate(thirds(t[kb:kb + 1]) + (jnp.zeros((5, rows), BF16),), axis=0)
        found += dot(cut, g2[kb])
    found = (found[2:3] + found[1:2]) + found[0:1]
    found = jnp.where(k == 0, found[:, :pairs], found[:, pairs:])
    prob_ref[...] = found[:, :part] + found[:, part:]

    def z_add(t, c):
        z_send(t).wait_recv()
        vol_ref[...] += zr[t].astype(F32)
        return c

    lax.fori_loop(0, nz - 1, z_add, 0)

    for e in ex:
        e.wait_send()
    facts_done.wait_send()
    remote(all_stat, all_stat, s_ss, s_rs, sibling).wait_send()
    remote(all_sums, all_sums, b_ss, b_rs, sibling).wait_send()
    prob_done.wait_send()
    for j in range(n_chunk):
        ref = recv.at[j, :, pl.ds(0, nq - 1)]
        remote(ref, ref, a_ss.at[j], a_rs.at[j], sibling).wait_send()
        sib_copy(j).wait_send()
    for j in range(nch):
        for way in range(2):
            y_copy(recv.at[j, k], piece(y, k, j), way, k, j).wait_send()
            y_copy(xs_all.at[piece(y, other, j)], piece(y, other, j), way, other, j).wait_send()
    for j in range(nch - far_n):
        f_copy(piece(y_dn, 0, j), 0, j).wait_send()
        f_copy(piece(y_up, 1, j), 1, j).wait_send()

    def v_done(t, c):
        sib_send(t).wait_send()
        x_all(t).wait_send()
        return c

    lax.fori_loop(0, nz, v_done, 0)
    lax.fori_loop(0, nz - 1, lambda t, c: (z_send(t).wait_send(), c)[1], 0)


def local(nz, images, bin_lists, precision, references, line_index, interp_blocks):
    ny, n_ptcl = lax.axis_size("cls"), lax.axis_size("ptcl")
    nq = n_ptcl // 2
    nx = nq // nz
    part, pixels = images.shape
    n_ref = references.shape[1]
    n_line = interp_blocks.shape[0]
    nch = pixels // (2 * ny * CW)
    n_chunk = nch + FAR
    rows = nq * 16
    nw = rows // 128
    vmem, dma = pltpu.VMEM, pltpu.SemaphoreType.DMA
    whole = pl.BlockSpec(memory_space=pltpu.VMEM)
    far = pl.BlockSpec(memory_space=pl.ANY)
    flops = 4 * n_ref * rows * pixels
    prob, volume = pl.pallas_call(
        functools.partial(kernel, ny, nx, nz, nch, FAR),
        out_shape=(jax.ShapeDtypeStruct((1, part), F32), jax.ShapeDtypeStruct((LINE, LINE), F32)),
        in_specs=[far, whole, whole, far, whole, far],
        out_specs=(whole, whole),
        scratch_shapes=[
            vmem((2, part, n_chunk * CW), BF16),
            vmem((2, 8, part), F32),
            vmem((2 * rows, 2 * part), BF16),
            vmem((2, rows, 4 * part), BF16),
            vmem((n_chunk, 2, nq, 16, CW), BF16),
            vmem((n_chunk, 2, nq, 16, CW), BF16),
            vmem((2 * ny * nch, nq, 16, CW), BF16),
            vmem((n_ref, pixels), BF16),
            vmem((n_line, LINE, n_ref), BF16),
            vmem((n_line, LINE, LINE), BF16),
            vmem((n_ref, rows), F32),
            vmem((n_ref, rows), BF16),
            vmem((n_ref, 128), F32),
            vmem((nw, 8, 128), F32), vmem((nq, 8, 128), F32),
            vmem((ny, 2, rows), F32),
            vmem((nw, 128), F32), vmem((n_ptcl, nw, 128), F32),
            vmem((nw, 1, 128), F32), vmem((n_ptcl, 1, 128), F32),
            vmem((nz, nx, 2, LINE, LINE), F32),
            vmem((nz, nx, LINE, LINE), F32),
            vmem((nz, nx - 1, LINE, LINE), BF16), vmem((nz, nx - 1, LINE, LINE), BF16),
            vmem((nz - 1, LINE, LINE), BF16), vmem((nz - 1, LINE, LINE), BF16),
            dma((4,)), dma((3,)), dma((3,)),
            dma((n_chunk,)), dma((n_chunk,)), dma((n_chunk,)),
            dma(()), dma(()),
            dma((n_chunk,)), dma((n_chunk,)), dma((n_chunk,)),
            dma((2, 2, nch)), dma((2, 2, nch)),
            dma((2, nch)), dma((2, nch)),
            dma(()), dma(()), dma(()), dma(()), dma(()), dma(()),
            dma((nz,)), dma((nz,)), dma((nz,)), dma((nz,)), dma((nz - 1,)), dma((nz - 1,)),
        ],
        compiler_params=pltpu.CompilerParams(collective_id=0, has_side_effects=True, vmem_limit_bytes=58 << 20),
        cost_estimate=pl.CostEstimate(flops=flops, bytes_accessed=n_ref * pixels * 2, transcendentals=0),
    )(images, bin_lists.T, precision.reshape(1, part), references[0], line_index[0].T, interp_blocks)
    return prob.reshape(part, 1), volume[None]


def solution(mesh, nz=NZ):
    in_specs = (
        P("ptcl", None),
        P("ptcl", None),
        P("ptcl"),
        P("cls", "ptcl", None),
        P("cls", "ptcl", None),
        P(),
    )
    out_specs = (P("ptcl", "cls"), P("cls", "ptcl", None))
    return jax.shard_map(functools.partial(local, nz), mesh=mesh, in_specs=in_specs, out_specs=out_specs,
                         check_vma=False)
```

```python
import functools

import jax
import jax.numpy as jnp
from jax import lax
from jax.experimental import pallas as pl
from jax.experimental.pallas import tpu as pltpu
from jax.sharding import PartitionSpec as P

MESH = pl.DeviceIdType.MESH
F32, BF16, I32 = jnp.float32, jnp.bfloat16, jnp.int32
NZ = 8
CW = 128
FAR = 4
LAG = 4
LINE = 128
SLOTS = 8


def iota(shape, dim):
    return lax.broadcasted_iota(I32, shape, dim)


def dot(a, b, ca=1, cb=0):
    return lax.dot_general(a, b, (((ca,), (cb,)), ((), ())), preferred_element_type=F32)


def thirds(v):
    hi = v.astype(BF16)
    rest = v - hi.astype(F32)
    mid = rest.astype(BF16)
    low = (rest - mid.astype(F32)).astype(BF16)
    return hi, mid, low


def kernel(ny, nx, nz, nd, far_n, img_hbm, bins_ref, prec_ref, refs_hbm, idx_hbm, interp_hbm, prob_ref, vol_ref,
           img, g, g2, sendbuf, recv, xs_all, refs, idx, onehot, interp, score, weight, hnorm,
           psend, ptab, stat, lrow, ltab, dsend, dtab, vb, sib, xs, xr, zs, zr,
           load_sem, a_ss, a_rs, a_loc, p_ss, p_rs,
           y_ss, y_rs, f_ss, f_rs, s_ss, s_rs, b_ss, b_rs, d_ss, d_rs,
           v_ss, v_rs, x_ss, x_rs, z_ss, z_rs):
    nq = nx * nz
    y, d = lax.axis_index("cls"), lax.axis_index("ptcl")
    q, k = d // 2, d % 2
    x, z = q // nz, q % nz
    other = 1 - k
    part = bins_ref.shape[1]
    n_bin, pairs = nq * 2, 2 * part
    n_pair = nd + far_n
    n_ref = refs.shape[0]
    rows = n_bin * SLOTS
    nw = rows // 128
    per_w = 128 // SLOTS
    sibling = (y, q * 2 + other)
    y_up, y_dn, y_far = (y + 1) % ny, (y + ny - 1) % ny, (y + 2) % ny
    up, dn = (y_up, d), (y_dn, d)

    def remote(src, dst, ss, rs, dev):
        return pltpu.make_async_remote_copy(src_ref=src, dst_ref=dst, send_sem=ss, recv_sem=rs,
                                            device_id=dev, device_id_type=MESH)

    def piece(yy, h, m):
        return (yy * nd + m) * 2 + h

    def pixels(p, count):
        return pl.ds(pl.multiple_of(p * CW, 2 * CW), count * CW)

    bar = pltpu.get_barrier_semaphore()

    def greet(i, c):
        pl.semaphore_signal(bar, inc=1, device_id=(y, (d + i) % n_bin), device_id_type=MESH)
        return c

    def greet_y(i, c):
        pl.semaphore_signal(bar, inc=1, device_id=((y + i) % ny, d), device_id_type=MESH)
        return c

    lax.fori_loop(1, n_bin, greet, 0)
    lax.fori_loop(1, ny, greet_y, 0)

    loads = [
        pltpu.make_async_copy(img_hbm.at[:, pixels(piece(y, 0, 0), 2 * nd)], img.at[:, pl.ds(0, 2 * nd * CW)],
                              load_sem.at[0]),
        pltpu.make_async_copy(img_hbm.at[:, pixels(piece(y_far, 0, nd - far_n), 2 * far_n)],
                              img.at[:, pl.ds(2 * nd * CW, 2 * far_n * CW)], load_sem.at[1]),
        pltpu.make_async_copy(idx_hbm, idx, load_sem.at[2]),
        pltpu.make_async_copy(refs_hbm, refs, load_sem.at[3]),
        pltpu.make_async_copy(interp_hbm, interp, load_sem.at[4]),
    ]
    for ld in loads:
        ld.start()

    own_bins = bins_ref[...].astype(F32)
    bins = jnp.concatenate([own_bins[0:1], own_bins[1:2]], axis=1)
    before = (iota((pairs, pairs), 0) < iota((pairs, pairs), 1)).astype(F32).astype(BF16)
    named = (iota((n_bin, pairs), 0).astype(F32) == bins).astype(F32)
    rank = named * dot(named.astype(BF16), before)
    expand = (lax.shift_right_logical(iota((rows, n_bin), 0), 3) == iota((rows, n_bin), 1)).astype(F32).astype(BF16)
    spread = dot(expand, (named + rank).astype(BF16))
    hit = (spread == ((iota((rows, pairs), 0) & 7) + 1).astype(F32)).astype(F32)
    g2[...] = hit.astype(BF16)
    g[...] = (hit[:, :part] + hit[:, part:]).astype(BF16)

    def gather(m):
        out = dot(g[...], img[:, 2 * m * CW:2 * (m + 1) * CW])
        halves = [out[:, h * CW:(h + 1) * CW].reshape(n_bin, SLOTS, CW) for h in range(2)]
        sendbuf[:, m] = jnp.concatenate(halves, axis=1).astype(BF16)

    def own_part(m, n, c):
        return pltpu.make_async_copy(sendbuf.at[d, pl.ds(m, n)], recv.at[d, pl.ds(m, n)], a_loc.at[c])

    def send_chunk(m, n, c):
        def send(i, carry):
            d2 = (d + i) % n_bin
            remote(sendbuf.at[d2, pl.ds(m, n)], recv.at[d, pl.ds(m, n)], a_ss.at[c], a_rs.at[c], (y, d2)).start()
            return carry

        lax.fori_loop(1, n_bin, send, 0)
        own_part(m, n, c).start()

    def chunk_all(m, n, c):
        ref = recv.at[pl.ds(0, n_bin - 1), pl.ds(m, n)]
        return remote(ref, ref, a_ss.at[c], a_rs.at[c], sibling)

    chunks = [(m, 1) for m in range(n_pair)]
    loads[0].wait()
    gather(0)
    pl.semaphore_wait(bar, n_bin - 1 + ny - 1)
    for c, (m, n) in enumerate(chunks):
        if c == nd:
            loads[1].wait()
        if c:
            gather(m)
        send_chunk(m, n, c)

    def own_lanes(t):
        axis = t.ndim - 1
        t = jnp.where(lax.shift_right_logical(iota(t.shape, axis), 3) == d % per_w, t, 0.0)
        for s in (64, 32, 16, 8):
            t = t + pltpu.roll(t, s, axis)
        return t

    def by_device(t):
        t = t.reshape(nw, per_w, t.shape[1], 128)
        return jnp.sum(jnp.where(lax.shift_right_logical(iota(t.shape, 3), 3) == iota(t.shape, 1), t, 0.0), axis=1)

    def in_row(t):
        return jnp.concatenate([t[w:w + 1] for w in range(nw)], axis=1)

    def in_windows(t):
        return jnp.concatenate([t[:, w * 128:(w + 1) * 128] for w in range(nw)], axis=0)

    prec = prec_ref[...].astype(F32)
    ranks = jnp.sum(rank, axis=0, keepdims=True)
    facts = [[prec, prec], [own_bins[1:2], own_bins[0:1]], [ranks[:, part:], ranks[:, :part]]]
    facts = [jnp.concatenate(v, axis=1) for v in facts]
    facts = jnp.concatenate(facts + [jnp.zeros((5, pairs), F32)], axis=0).astype(BF16)
    facts = dot(facts, g2[...], 1, 1)
    facts = jnp.concatenate([facts[0:1], facts[1:2] * SLOTS + facts[2:3]], axis=0)
    for w in range(nw):
        psend[w] = facts[:, w * 128:(w + 1) * 128]

    def send_facts(i, c):
        d2 = (d + i) % n_bin
        remote(psend.at[d2 // per_w], ptab.at[d], p_ss, p_rs, (y, d2)).start()
        return c

    lax.fori_loop(1, n_bin, send_facts, 0)
    ptab[d] = psend[d // per_w]
    facts_done = remote(ptab.at[pl.ds(0, n_bin - 1)], ptab.at[pl.ds(0, n_bin - 1)], p_ss, p_rs, sibling)

    hnorm[...] = jnp.zeros_like(hnorm)
    score[...] = jnp.zeros_like(score)

    def aside(m):
        def norm(i, c):
            v = refs[:, pl.ds(pl.multiple_of(i * 128, 128), 128)].astype(F32)
            hnorm[...] += v * v
            return c

        def bands(i, c):
            onehot[i] = (iota((LINE, n_ref), 0) == idx[pl.ds(i, 1), :]).astype(F32).astype(BF16)
            return c

        count = onehot.shape[0] // nd
        lax.fori_loop(m * count, (m + 1) * count, norm, 0)
        lax.fori_loop(m * count, (m + 1) * count, bands, 0)

    def slab(p):
        return jnp.concatenate([xs_all[p].reshape(rows, CW), xs_all[p + 1].reshape(rows, CW)], axis=1)

    def add_score(p):
        score[...] += dot(refs[:, pixels(p, 2)], slab(p), 1, 1)

    def y_copy(way, h, m):
        ref = xs_all.at[piece(y, h, m)]
        return remote(ref, ref, y_ss.at[way, h, m], y_rs.at[way, h, m], up if way == 0 else dn)

    def f_copy(way, m):
        ref = xs_all.at[piece(y_dn if way == 0 else y_up, way, m)]
        return remote(ref, ref, f_ss.at[way, m], f_rs.at[way, m], up if way == 0 else dn)

    def stage0(c):
        m, n = chunks[c]
        chunk_all(m, n, c).wait_recv()
        own_part(m, n, c).wait()
        for i in range(m, m + n):
            t = recv[:, i].astype(F32)
            for h in range(2):
                p = piece(y, h, i) if i < nd else piece(y_far, h, i - far_n)
                xs_all[p] = t[:, h * SLOTS:(h + 1) * SLOTS].reshape(nq, 16, CW).astype(BF16)
            if i < nd:
                for h in range(2):
                    for way in range(2):
                        y_copy(way, h, i).start()

    def stage1(m):
        for way in range(2):
            y_copy(way, way, m).wait_recv()
            if m < nd - far_n:
                f_copy(way, m).start()
        add_score(piece(y, 0, m))
        for way in range(2):
            y_copy(way, 1 - way, m).wait_recv()
        add_score(piece(y_dn, 0, m))
        add_score(piece(y_up, 0, m))

    def stage2(m):
        if m < nd - far_n:
            for way in range(2):
                f_copy(way, m).wait_recv()
        add_score(piece(y_far, 0, m))

    loads[2].wait()
    loads[3].wait()
    for m in range(nd):
        stage0(m)
        if m >= 1:
            stage1(m - 1)
        if 2 <= m < nd - far_n + 2:
            stage2(m - 2)
        aside(m)
    stage1(nd - 1)
    for c in range(nd, n_pair):
        stage0(c)
    for m in range(min(nd - 2, nd - far_n), nd):
        stage2(m)

    facts_done.wait_recv()
    known = by_device(own_lanes(ptab[...]))
    scale = in_row(known[:, 0])
    mate = known[:, 1]
    half = 0.5 * jnp.sum(hnorm[...], axis=1, keepdims=True)
    s = scale * (score[...] - half)
    score[...] = s
    top = jnp.max(s, axis=0, keepdims=True)
    total = jnp.sum(jnp.exp(s - top), axis=0, keepdims=True)
    stat[y] = jnp.concatenate([top, total], axis=0)

    def share(i, c):
        remote(stat.at[y], stat.at[y], s_ss, s_rs, ((y + i) % ny, d)).start()
        return c

    lax.fori_loop(1, ny, share, 0)
    all_stat = stat.at[pl.ds(0, ny - 1)]
    remote(all_stat, all_stat, s_ss, s_rs, sibling).wait_recv()
    tops = [stat[yy, 0:1] for yy in range(ny)]
    high = functools.reduce(jnp.maximum, tops)
    mine = in_windows(high + jnp.log(sum(stat[yy, 1:2] * jnp.exp(tops[yy] - high) for yy in range(ny))))

    lrow[...] = mine

    def spread_sums(i, c):
        remote(lrow, ltab.at[d], b_ss, b_rs, (y, (d + i) % n_bin)).start()
        return c

    lax.fori_loop(1, n_bin, spread_sums, 0)
    ltab[d] = mine
    all_sums = ltab.at[pl.ds(0, n_bin - 1)]
    remote(all_sums, all_sums, b_ss, b_rs, sibling).wait_recv()
    sums = ltab[...]
    slot = iota((nw, 128), 1) & 7
    key = (iota(sums.shape, 0) * SLOTS + (iota(sums.shape, 2) & 7)).astype(F32)
    theirs = jnp.zeros((nw, 128), F32)
    for delta in range(1 - SLOTS, SLOTS):
        asked = pltpu.roll(mate, delta % 128, 1)
        asked = jnp.where((slot - delta >= 0) & (slot - delta < SLOTS), asked, -1.0)
        found = jnp.sum(jnp.where(key == asked[None], sums, 0.0), axis=0)
        theirs = theirs + pltpu.roll(found, (-delta) % 128, 1)
    high = jnp.maximum(mine, theirs)
    log = in_row(high + jnp.log(jnp.exp(mine - high) + jnp.exp(theirs - high)))
    weight[...] = (n_ref * jnp.exp(score[...] - log)).astype(BF16)

    loads[4].wait()

    def sib_send(t):
        return remote(vb.at[t, :, other], sib.at[t], v_ss.at[t], v_rs.at[t], sibling)

    def x_send(t, i):
        x2 = (x + nx - 1 - i) % nx
        return remote(xs.at[t, i], xr.at[t, i], x_ss.at[t], x_rs.at[t], (y, (x2 * nz + z) * 2 + k))

    def x_all(t):
        ref = xr.at[t]
        return remote(ref, ref, x_ss.at[t], x_rs.at[t], sibling)

    def z_send(t):
        z2 = (z + nz - 1 - t) % nz
        return remote(zs.at[t], zr.at[t], z_ss.at[t], z_rs.at[t], (y, (x * nz + z2) * 2 + k))

    def insert(t):
        chips = [((x + nx - 1 - i) % nx) * nz + (z + nz - 1 - t) % nz for i in range(nx)]
        images = [dot(weight[...], slab(2 * c)).astype(BF16) for c in chips]
        sums = [dot(onehot[2 * c + h], im[:, h * LINE:(h + 1) * LINE]) for c, im in zip(chips, images) for h in (0, 1)]
        out = []
        for i in range(nx):
            for h in range(2):
                band = sums[2 * i + h]
                hi = band.astype(BF16)
                low = (band - hi.astype(F32)).astype(BF16)
                block = interp[2 * chips[i] + h]
                out.append(dot(jnp.concatenate([hi, low], axis=1), jnp.concatenate([block, block], axis=0)))
        for i in range(nx):
            for h in range(2):
                vb[t, i, h] = out[2 * i + h]

    def step(t, c):
        @pl.when(t < nz)
        def _():
            insert(t)
            sib_send(t).start()

        @pl.when((t >= 1) & (t <= nz))
        def _():
            u = t - 1
            sib_send(u).wait_recv()

            def one(i, c):
                xs[u, i] = (vb[u, i, k] + sib[u, i]).astype(BF16)
                x_send(u, i).start()
                return c

            lax.fori_loop(0, nx - 1, one, 0)

        @pl.when(t >= LAG)
        def _():
            u = t - LAG
            x_all(u).wait_recv()
            total = vb[u, nx - 1, k] + sib[u, nx - 1]
            for i in range(nx - 1):
                total += xr[u, i].astype(F32)

            @pl.when(u < nz - 1)
            def _():
                zs[u] = total.astype(BF16)
                z_send(u).start()

            @pl.when(u == nz - 1)
            def _():
                vol_ref[...] = total

        return c

    lax.fori_loop(0, 2, step, 0)

    chance = stat[y][1:2] * jnp.exp(stat[y][0:1] - log)
    for w in range(nw):
        dsend[w] = chance[:, w * 128:(w + 1) * 128]

    def send_prob(i, c):
        d2 = (d + i) % n_bin
        remote(dsend.at[d2 // per_w], dtab.at[d], d_ss, d_rs, (y, d2)).start()
        return c

    lax.fori_loop(1, n_bin, send_prob, 0)
    dtab[d] = dsend[d // per_w]
    prob_done = remote(dtab.at[pl.ds(0, n_bin - 1)], dtab.at[pl.ds(0, n_bin - 1)], d_ss, d_rs, sibling)

    lax.fori_loop(2, nz + 1, step, 0)

    prob_done.wait_recv()
    found = in_row(by_device(own_lanes(dtab[...]))[:, 0])
    found = dot(jnp.concatenate(thirds(found) + (jnp.zeros((5, rows), BF16),), axis=0), g2[...])
    found = (found[2:3] + found[1:2]) + found[0:1]
    prob_ref[...] = found[:, :part] + found[:, part:]

    lax.fori_loop(nz + 1, nz + LAG, step, 0)

    def z_add(t, c):
        z_send(t).wait_recv()
        vol_ref[...] += zr[t].astype(F32)
        return c

    lax.fori_loop(0, nz - 1, z_add, 0)

    facts_done.wait_send()
    remote(all_stat, all_stat, s_ss, s_rs, sibling).wait_send()
    remote(all_sums, all_sums, b_ss, b_rs, sibling).wait_send()
    prob_done.wait_send()
    for c, (m, n) in enumerate(chunks):
        chunk_all(m, n, c).wait_send()
    for m in range(nd):
        for way in range(2):
            for h in range(2):
                y_copy(way, h, m).wait_send()
            if m < nd - far_n:
                f_copy(way, m).wait_send()

    def v_done(t, c):
        sib_send(t).wait_send()
        x_all(t).wait_send()
        return c

    lax.fori_loop(0, nz, v_done, 0)
    lax.fori_loop(0, nz - 1, lambda t, c: (z_send(t).wait_send(), c)[1], 0)


def local(nz, images, bin_lists, precision, references, line_index, interp_blocks):
    ny, n_ptcl = lax.axis_size("cls"), lax.axis_size("ptcl")
    nq = n_ptcl // 2
    nx = nq // nz
    part, pixels = images.shape
    n_ref = references.shape[1]
    n_line = interp_blocks.shape[0]
    nd = pixels // (2 * ny * CW)
    n_pair = nd + FAR
    rows = n_ptcl * SLOTS
    nw = rows // 128
    vmem, dma = pltpu.VMEM, pltpu.SemaphoreType.DMA
    whole = pl.BlockSpec(memory_space=pltpu.VMEM)
    far = pl.BlockSpec(memory_space=pl.ANY)
    flops = 4 * n_ref * rows * pixels
    prob, volume = pl.pallas_call(
        functools.partial(kernel, ny, nx, nz, nd, FAR),
        out_shape=(jax.ShapeDtypeStruct((1, part), F32), jax.ShapeDtypeStruct((LINE, LINE), F32)),
        in_specs=[far, whole, whole, far, far, far],
        out_specs=(whole, whole),
        scratch_shapes=[
            vmem((part, 2 * n_pair * CW), BF16),
            vmem((rows, part), BF16),
            vmem((rows, 2 * part), BF16),
            vmem((n_ptcl, n_pair, 16, CW), BF16),
            vmem((n_ptcl, n_pair, 16, CW), BF16),
            vmem((2 * ny * nd, nq, 16, CW), BF16),
            vmem((n_ref, pixels), BF16),
            vmem((n_line, n_ref), I32),
            vmem((n_line, LINE, n_ref), BF16),
            vmem((n_line, LINE, LINE), BF16),
            vmem((n_ref, rows), F32),
            vmem((n_ref, rows), BF16),
            vmem((n_ref, 128), F32),
            vmem((nw, 2, 128), F32), vmem((n_ptcl, 2, 128), F32),
            vmem((ny, 2, rows), F32),
            vmem((nw, 128), F32), vmem((n_ptcl, nw, 128), F32),
            vmem((nw, 1, 128), F32), vmem((n_ptcl, 1, 128), F32),
            vmem((nz, nx, 2, LINE, LINE), F32),
            vmem((nz, nx, LINE, LINE), F32),
            vmem((nz, nx - 1, LINE, LINE), BF16), vmem((nz, nx - 1, LINE, LINE), BF16),
            vmem((nz - 1, LINE, LINE), BF16), vmem((nz - 1, LINE, LINE), BF16),
            dma((5,)),
            dma((n_pair,)), dma((n_pair,)), dma((n_pair,)),
            dma(()), dma(()),
            dma((2, 2, nd)), dma((2, 2, nd)),
            dma((2, nd)), dma((2, nd)),
            dma(()), dma(()), dma(()), dma(()), dma(()), dma(()),
            dma((nz,)), dma((nz,)), dma((nz,)), dma((nz,)), dma((nz - 1,)), dma((nz - 1,)),
        ],
        compiler_params=pltpu.CompilerParams(collective_id=0, has_side_effects=True, vmem_limit_bytes=58 << 20),
        cost_estimate=pl.CostEstimate(flops=flops, bytes_accessed=n_ref * pixels * 2, transcendentals=0),
    )(images, bin_lists.T, precision.reshape(1, part), references[0], line_index[0].T, interp_blocks)
    return prob.reshape(part, 1), volume[None]


def solution(mesh, nz=NZ):
    in_specs = (
        P("ptcl", None),
        P("ptcl", None),
        P("ptcl"),
        P("cls", "ptcl", None),
        P("cls", "ptcl", None),
        P(),
    )
    out_specs = (P("ptcl", "cls"), P("cls", "ptcl", None))
    return jax.shard_map(functools.partial(local, nz), mesh=mesh, in_specs=in_specs, out_specs=out_specs,
                         check_vma=False)
```

```python
import functools

import jax
import jax.numpy as jnp
from jax import lax
from jax.experimental import pallas as pl
from jax.experimental.pallas import tpu as pltpu
from jax.sharding import PartitionSpec as P

MESH = pl.DeviceIdType.MESH
F32, BF16, I32 = jnp.float32, jnp.bfloat16, jnp.int32
NZ = 8
CW = 128
FAR = 4
HOLD = 2
LAG = 5
AHEAD = 5
LINE = 128
SLOTS = 8


def iota(shape, dim):
    return lax.broadcasted_iota(I32, shape, dim)


def dot(a, b, ca=1, cb=0):
    return lax.dot_general(a, b, (((ca,), (cb,)), ((), ())), preferred_element_type=F32)


def thirds(v):
    hi = v.astype(BF16)
    rest = v - hi.astype(F32)
    mid = rest.astype(BF16)
    low = (rest - mid.astype(F32)).astype(BF16)
    return hi, mid, low


def kernel(ny, nx, nz, nd, far_n, img_hbm, bins_hbm, prec_hbm, refs_hbm, idx_hbm, interp_hbm, prob_ref, vol_ref,
           img, bins_ref, prec_ref, g, g2, sendbuf, recv, xs_all, refs, idx, onehot, interp, score, weight, hnorm,
           psend, ptab, stat, lrow, ltab, dsend, dtab, vb, sib, xs, xr, zs, zr,
           load_sem, a_ss, a_rs, a_loc, h_ss, h_rs, p_ss, p_rs,
           y_ss, y_rs, f_ss, f_rs, s_ss, s_rs, b_ss, b_rs, d_ss, d_rs,
           v_ss, v_rs, x_ss, x_rs, z_ss, z_rs):
    nq = nx * nz
    y, d = lax.axis_index("cls"), lax.axis_index("ptcl")
    q, k = d // 2, d % 2
    x, z = q // nz, q % nz
    other = 1 - k
    part = bins_ref.shape[1]
    n_bin, pairs = nq * 2, 2 * part
    n_pair = nd + far_n
    n_ref = refs.shape[0]
    rows = n_bin * SLOTS
    nw = rows // 128
    per_w = 128 // SLOTS
    sibling = (y, q * 2 + other)
    y_up, y_dn, y_far = (y + 1) % ny, (y + ny - 1) % ny, (y + 2) % ny
    up, dn = (y_up, d), (y_dn, d)

    def remote(src, dst, ss, rs, dev):
        return pltpu.make_async_remote_copy(src_ref=src, dst_ref=dst, send_sem=ss, recv_sem=rs,
                                            device_id=dev, device_id_type=MESH)

    def piece(yy, h, m):
        return (yy * nd + m) * 2 + h

    def pixels(p, count):
        return pl.ds(pl.multiple_of(p * CW, 2 * CW), count * CW)

    bar = pltpu.get_barrier_semaphore()

    def greet(i, c):
        pl.semaphore_signal(bar, inc=1, device_id=(y, (d + i) % n_bin), device_id_type=MESH)
        return c

    def greet_y(i, c):
        pl.semaphore_signal(bar, inc=1, device_id=((y + i) % ny, d), device_id_type=MESH)
        return c

    lax.fori_loop(1, n_bin, greet, 0)
    lax.fori_loop(1, ny, greet_y, 0)

    loads = [
        pltpu.make_async_copy(img_hbm.at[:, pixels(piece(y, 0, 1), 2 * nd - 2)],
                              img.at[:, pl.ds(2 * CW, (2 * nd - 2) * CW)], load_sem.at[0]),
        pltpu.make_async_copy(img_hbm.at[:, pixels(piece(y_far, 0, nd - far_n), 2 * far_n)],
                              img.at[:, pl.ds(2 * nd * CW, 2 * far_n * CW)], load_sem.at[1]),
        pltpu.make_async_copy(idx_hbm, idx, load_sem.at[2]),
        pltpu.make_async_copy(refs_hbm, refs, load_sem.at[3]),
        pltpu.make_async_copy(interp_hbm, interp, load_sem.at[4]),
    ]
    first = [
        pltpu.make_async_copy(bins_hbm, bins_ref, load_sem.at[5]),
        pltpu.make_async_copy(img_hbm.at[:, pixels(piece(y, 0, 0), 2)], img.at[:, pl.ds(0, 2 * CW)], load_sem.at[6]),
        pltpu.make_async_copy(prec_hbm, prec_ref, load_sem.at[7]),
    ]
    for ld in first + loads:
        ld.start()

    first[0].wait()
    own_bins = bins_ref[...].astype(F32)
    bins = jnp.concatenate([own_bins[0:1], own_bins[1:2]], axis=1)
    before = (iota((pairs, pairs), 0) < iota((pairs, pairs), 1)).astype(F32).astype(BF16)
    named = (iota((n_bin, pairs), 0).astype(F32) == bins).astype(F32)
    rank = named * dot(named.astype(BF16), before)
    expand = (lax.shift_right_logical(iota((rows, n_bin), 0), 3) == iota((rows, n_bin), 1)).astype(F32).astype(BF16)
    spread = dot(expand, (named + rank).astype(BF16))
    hit = (spread == ((iota((rows, pairs), 0) & 7) + 1).astype(F32)).astype(F32)
    g2[...] = hit.astype(BF16)
    g[...] = (hit[:, :part] + hit[:, part:]).astype(BF16)

    def gather(m):
        out = dot(g[...], img[:, 2 * m * CW:2 * (m + 1) * CW])
        halves = [out[:, h * CW:(h + 1) * CW].reshape(n_bin, SLOTS, CW) for h in range(2)]
        sendbuf[:, m] = jnp.concatenate(halves, axis=1).astype(BF16)

    def own_part(m, n, c):
        return pltpu.make_async_copy(sendbuf.at[d, pl.ds(m, n)], recv.at[d, pl.ds(m, n)], a_loc.at[c])

    def send_chunk(m, n, c):
        def send(i, carry):
            d2 = (d + i) % n_bin
            remote(sendbuf.at[d2, pl.ds(m, n)], recv.at[d, pl.ds(m, n)], a_ss.at[c], a_rs.at[c], (y, d2)).start()
            return carry

        lax.fori_loop(1, n_bin, send, 0)
        own_part(m, n, c).start()

    def chunk_all(m, n, c):
        ref = recv.at[pl.ds(0, n_bin - 1), pl.ds(m, n)]
        return remote(ref, ref, a_ss.at[c], a_rs.at[c], sibling)

    group = 2 * nz
    steps_x = sorted(range(nx), key=lambda dx: min(dx, nx - dx))

    def send_head(dx):
        def send(i, carry):
            d2 = ((x + dx) % nx) * group + (d + i) % group
            remote(sendbuf.at[d2, pl.ds(0, 1)], recv.at[d, pl.ds(0, 1)], h_ss.at[dx], h_rs.at[dx], (y, d2)).start()
            return carry

        lax.fori_loop(0 if dx else 1, group, send, 0)

    def head_all(dx):
        ref = recv.at[pl.ds(0, group if dx else group - 1), pl.ds(0, 1)]
        return remote(ref, ref, h_ss.at[dx], h_rs.at[dx], sibling)

    chunks = [(m, 1) for m in range(n_pair)]
    first[1].wait()
    gather(0)
    pl.semaphore_wait(bar, n_bin - 1 + ny - 1)

    def issue(c):
        m, n = chunks[c]
        if c == 1:
            loads[0].wait()
        if c == nd:
            loads[1].wait()
        gather(m)
        send_chunk(m, n, c)

    own_part(0, 1, 0).start()
    for dx in steps_x:
        send_head(dx)
    for c in range(1, min(AHEAD, n_pair)):
        issue(c)

    def own_lanes(t):
        axis = t.ndim - 1
        t = jnp.where(lax.shift_right_logical(iota(t.shape, axis), 3) == d % per_w, t, 0.0)
        for s in (64, 32, 16, 8):
            t = t + pltpu.roll(t, s, axis)
        return t

    def by_device(t):
        t = t.reshape(nw, per_w, t.shape[1], 128)
        return jnp.sum(jnp.where(lax.shift_right_logical(iota(t.shape, 3), 3) == iota(t.shape, 1), t, 0.0), axis=1)

    def in_row(t):
        return jnp.concatenate([t[w:w + 1] for w in range(nw)], axis=1)

    def in_windows(t):
        return jnp.concatenate([t[:, w * 128:(w + 1) * 128] for w in range(nw)], axis=0)

    first[2].wait()
    prec = prec_ref[...].astype(F32)
    ranks = jnp.sum(rank, axis=0, keepdims=True)
    facts = [[prec, prec], [own_bins[1:2], own_bins[0:1]], [ranks[:, part:], ranks[:, :part]]]
    facts = [jnp.concatenate(v, axis=1) for v in facts]
    facts = jnp.concatenate(facts + [jnp.zeros((5, pairs), F32)], axis=0).astype(BF16)
    facts = dot(facts, g2[...], 1, 1)
    facts = jnp.concatenate([facts[0:1], facts[1:2] * SLOTS + facts[2:3]], axis=0)
    for w in range(nw):
        psend[w] = facts[:, w * 128:(w + 1) * 128]

    def send_facts(i, c):
        d2 = (d + i) % n_bin
        remote(psend.at[d2 // per_w], ptab.at[d], p_ss, p_rs, (y, d2)).start()
        return c

    lax.fori_loop(1, n_bin, send_facts, 0)
    ptab[d] = psend[d // per_w]
    facts_done = remote(ptab.at[pl.ds(0, n_bin - 1)], ptab.at[pl.ds(0, n_bin - 1)], p_ss, p_rs, sibling)

    hnorm[...] = jnp.zeros_like(hnorm)
    score[...] = jnp.zeros_like(score)

    def aside(m):
        def norm(i, c):
            v = refs[:, pl.ds(pl.multiple_of(i * 128, 128), 128)].astype(F32)
            hnorm[...] += v * v
            return c

        def bands(i, c):
            onehot[i] = (iota((LINE, n_ref), 0) == idx[pl.ds(i, 1), :]).astype(F32).astype(BF16)
            return c

        count = onehot.shape[0] // nd
        lax.fori_loop(m * count, (m + 1) * count, norm, 0)
        lax.fori_loop(m * count, (m + 1) * count, bands, 0)

    def slab(p):
        return jnp.concatenate([xs_all[p].reshape(rows, CW), xs_all[p + 1].reshape(rows, CW)], axis=1)

    def add_score(p):
        score[...] += dot(refs[:, pixels(p, 2)], slab(p), 1, 1)

    def y_copy(way, h, m):
        ref = xs_all.at[piece(y, h, m)]
        return remote(ref, ref, y_ss.at[way, h, m], y_rs.at[way, h, m], up if way == 0 else dn)

    def f_copy(way, m):
        ref = xs_all.at[piece(y_dn if way == 0 else y_up, way, m)]
        return remote(ref, ref, f_ss.at[way, m], f_rs.at[way, m], up if way == 0 else dn)

    def stage0(c):
        m, n = chunks[c]
        chunk_all(m, n, c).wait_recv()
        own_part(m, n, c).wait()
        for i in range(m, m + n):
            t = recv[:, i].astype(F32)
            for h in range(2):
                p = piece(y, h, i) if i < nd else piece(y_far, h, i - far_n)
                xs_all[p] = t[:, h * SLOTS:(h + 1) * SLOTS].reshape(nq, 16, CW).astype(BF16)
            if i < nd:
                for h in range(2):
                    for way in range(2):
                        y_copy(way, h, i).start()
        if c + AHEAD - 1 < n_pair:
            issue(c + AHEAD - 1)

    def head_copy(way, h, x_src):
        ref = xs_all.at[piece(y, h, 0), pl.ds(x_src * nz, nz)]
        return remote(ref, ref, y_ss.at[way, h, 0], y_rs.at[way, h, 0], up if way == 0 else dn)

    def stage_head():
        own_part(0, 1, 0).wait()
        for dx in steps_x:
            head_all(dx).wait_recv()
            x_src = (x + nx - dx) % nx
            t = recv[pl.ds(x_src * group, group), 0].astype(F32)
            for h in range(2):
                xs_all[piece(y, h, 0), pl.ds(x_src * nz, nz)] = (
                    t[:, h * SLOTS:(h + 1) * SLOTS].reshape(nz, 16, CW).astype(BF16))
                for way in range(2):
                    head_copy(way, h, x_src).start()

    def stage1(m):
        for way in range(2):
            y_copy(way, way, m).wait_recv()
            if m < nd - far_n:
                f_copy(way, m).start()
        add_score(piece(y, 0, m))
        for way in range(2):
            y_copy(way, 1 - way, m).wait_recv()
        add_score(piece(y_dn, 0, m))
        add_score(piece(y_up, 0, m))

    def stage2(m):
        if m < nd - far_n:
            for way in range(2):
                f_copy(way, m).wait_recv()
        add_score(piece(y_far, 0, m))

    loads[2].wait()
    loads[3].wait()
    for m in range(nd):
        if m:
            stage0(m)
        else:
            stage_head()
        if m >= 1:
            stage1(m - 1)
        if 2 <= m < nd - far_n + 2:
            stage2(m - 2)
        aside(m)
    score[...] -= 0.5 * jnp.sum(hnorm[...], axis=1, keepdims=True)
    facts_done.wait_recv()
    known = by_device(own_lanes(ptab[...]))
    scale = in_row(known[:, 0])
    mate = known[:, 1]
    stage1(nd - 1)
    for m in range(nd - 2, nd - far_n):
        stage2(m)
    for c in range(nd, n_pair):
        stage0(c)
        stage2(c - far_n)

    s = scale * score[...]
    score[...] = s
    top = jnp.max(s, axis=0, keepdims=True)
    total = jnp.sum(jnp.exp(s - top), axis=0, keepdims=True)
    stat[y] = jnp.concatenate([top, total], axis=0)

    def share(i, c):
        remote(stat.at[y], stat.at[y], s_ss, s_rs, ((y + i) % ny, d)).start()
        return c

    lax.fori_loop(1, ny, share, 0)
    all_stat = stat.at[pl.ds(0, ny - 1)]
    remote(all_stat, all_stat, s_ss, s_rs, sibling).wait_recv()
    tops = [stat[yy, 0:1] for yy in range(ny)]
    high = functools.reduce(jnp.maximum, tops)
    mine = in_windows(high + jnp.log(sum(stat[yy, 1:2] * jnp.exp(tops[yy] - high) for yy in range(ny))))

    lrow[...] = mine

    def spread_sums(i, c):
        remote(lrow, ltab.at[d], b_ss, b_rs, (y, (d + i) % n_bin)).start()
        return c

    lax.fori_loop(1, n_bin, spread_sums, 0)
    ltab[d] = mine
    all_sums = ltab.at[pl.ds(0, n_bin - 1)]
    remote(all_sums, all_sums, b_ss, b_rs, sibling).wait_recv()
    sums = ltab[...]
    slot = iota((nw, 128), 1) & 7
    key = (iota(sums.shape, 0) * SLOTS + (iota(sums.shape, 2) & 7)).astype(F32)
    theirs = jnp.zeros((nw, 128), F32)
    for delta in range(1 - SLOTS, SLOTS):
        asked = pltpu.roll(mate, delta % 128, 1)
        asked = jnp.where((slot - delta >= 0) & (slot - delta < SLOTS), asked, -1.0)
        found = jnp.sum(jnp.where(key == asked[None], sums, 0.0), axis=0)
        theirs = theirs + pltpu.roll(found, (-delta) % 128, 1)
    high = jnp.maximum(mine, theirs)
    log = in_row(high + jnp.log(jnp.exp(mine - high) + jnp.exp(theirs - high)))
    weight[...] = (n_ref * jnp.exp(score[...] - log)).astype(BF16)

    loads[4].wait()

    def sib_send(t):
        return remote(vb.at[t, :, other], sib.at[t], v_ss.at[t], v_rs.at[t], sibling)

    def x_send(t, i):
        x2 = (x + nx - 1 - i) % nx
        return remote(xs.at[t, i], xr.at[t, i], x_ss.at[t], x_rs.at[t], (y, (x2 * nz + z) * 2 + k))

    def x_all(t):
        ref = xr.at[t]
        return remote(ref, ref, x_ss.at[t], x_rs.at[t], sibling)

    def z_send(t):
        z2 = (z + nz - 1 - t) % nz
        return remote(zs.at[t], zr.at[t], z_ss.at[t], z_rs.at[t], (y, (x * nz + z2) * 2 + k))

    def insert(t):
        chips = [((x + nx - 1 - i) % nx) * nz + (z + nz - 1 - t) % nz for i in range(nx)]
        images = [dot(weight[...], slab(2 * c)).astype(BF16) for c in chips]
        sums = [dot(onehot[2 * c + h], im[:, h * LINE:(h + 1) * LINE]) for c, im in zip(chips, images) for h in (0, 1)]
        out = []
        for i in range(nx):
            for h in range(2):
                band = sums[2 * i + h]
                hi = band.astype(BF16)
                low = (band - hi.astype(F32)).astype(BF16)
                block = interp[2 * chips[i] + h]
                out.append(dot(jnp.concatenate([hi, low], axis=1), jnp.concatenate([block, block], axis=0)))
        for i in range(nx):
            for h in range(2):
                vb[t, i, h] = out[2 * i + h]

    def step(t, c):
        @pl.when(t < nz)
        def _():
            insert(t)
            sib_send(t).start()

        @pl.when((t >= HOLD) & (t < nz + HOLD))
        def _():
            u = t - HOLD
            sib_send(u).wait_recv()

            def one(i, c):
                xs[u, i] = (vb[u, i, k] + sib[u, i]).astype(BF16)
                x_send(u, i).start()
                return c

            lax.fori_loop(0, nx - 1, one, 0)

        @pl.when(t >= LAG)
        def _():
            u = t - LAG
            x_all(u).wait_recv()
            total = vb[u, nx - 1, k] + sib[u, nx - 1]
            for i in range(nx - 1):
                total += xr[u, i].astype(F32)

            @pl.when(u < nz - 1)
            def _():
                zs[u] = total.astype(BF16)
                z_send(u).start()

            @pl.when(u == nz - 1)
            def _():
                vol_ref[...] = total

        return c

    lax.fori_loop(0, 2, step, 0)

    chance = stat[y][1:2] * jnp.exp(stat[y][0:1] - log)
    for w in range(nw):
        dsend[w] = chance[:, w * 128:(w + 1) * 128]

    def send_prob(i, c):
        d2 = (d + i) % n_bin
        remote(dsend.at[d2 // per_w], dtab.at[d], d_ss, d_rs, (y, d2)).start()
        return c

    lax.fori_loop(1, n_bin, send_prob, 0)
    dtab[d] = dsend[d // per_w]
    prob_done = remote(dtab.at[pl.ds(0, n_bin - 1)], dtab.at[pl.ds(0, n_bin - 1)], d_ss, d_rs, sibling)

    lax.fori_loop(2, nz + HOLD, step, 0)

    prob_done.wait_recv()
    found = in_row(by_device(own_lanes(dtab[...]))[:, 0])
    found = dot(jnp.concatenate(thirds(found) + (jnp.zeros((5, rows), BF16),), axis=0), g2[...])
    found = (found[2:3] + found[1:2]) + found[0:1]
    prob_ref[...] = found[:, :part] + found[:, part:]

    lax.fori_loop(nz + HOLD, nz + LAG, step, 0)

    def z_add(t, c):
        z_send(t).wait_recv()
        vol_ref[...] += zr[t].astype(F32)
        return c

    lax.fori_loop(0, nz - 1, z_add, 0)

    facts_done.wait_send()
    remote(all_stat, all_stat, s_ss, s_rs, sibling).wait_send()
    remote(all_sums, all_sums, b_ss, b_rs, sibling).wait_send()
    prob_done.wait_send()
    for dx in steps_x:
        head_all(dx).wait_send()
    for c, (m, n) in enumerate(chunks):
        if c:
            chunk_all(m, n, c).wait_send()
    for m in range(nd):
        for way in range(2):
            for h in range(2):
                y_copy(way, h, m).wait_send()
            if m < nd - far_n:
                f_copy(way, m).wait_send()

    def v_done(t, c):
        sib_send(t).wait_send()
        x_all(t).wait_send()
        return c

    lax.fori_loop(0, nz, v_done, 0)
    lax.fori_loop(0, nz - 1, lambda t, c: (z_send(t).wait_send(), c)[1], 0)


def hand_on(a_ref, b_ref, c_ref, d_ref):
    c_ref[...] = a_ref[...]
    d_ref[...] = b_ref[...]


def local(nz, images, bin_lists, precision, references, line_index, interp_blocks):
    ny, n_ptcl = lax.axis_size("cls"), lax.axis_size("ptcl")
    nq = n_ptcl // 2
    nx = nq // nz
    part, pixels = images.shape
    n_ref = references.shape[1]
    n_line = interp_blocks.shape[0]
    nd = pixels // (2 * ny * CW)
    n_pair = nd + FAR
    rows = n_ptcl * SLOTS
    nw = rows // 128
    vmem, dma = pltpu.VMEM, pltpu.SemaphoreType.DMA
    whole = pl.BlockSpec(memory_space=pltpu.VMEM)
    far = pl.BlockSpec(memory_space=pl.ANY)
    flops = 4 * n_ref * rows * pixels
    prob, volume = pl.pallas_call(
        functools.partial(kernel, ny, nx, nz, nd, FAR),
        out_shape=(jax.ShapeDtypeStruct((1, part), F32), jax.ShapeDtypeStruct((LINE, LINE), F32)),
        in_specs=[far] * 6,
        out_specs=(whole, whole),
        scratch_shapes=[
            vmem((part, 2 * n_pair * CW), BF16),
            vmem((2, part), I32),
            vmem((1, part), BF16),
            vmem((rows, part), BF16),
            vmem((rows, 2 * part), BF16),
            vmem((n_ptcl, n_pair, 16, CW), BF16),
            vmem((n_ptcl, n_pair, 16, CW), BF16),
            vmem((2 * ny * nd, nq, 16, CW), BF16),
            vmem((n_ref, pixels), BF16),
            vmem((n_line, n_ref), I32),
            vmem((n_line, LINE, n_ref), BF16),
            vmem((n_line, LINE, LINE), BF16),
            vmem((n_ref, rows), F32),
            vmem((n_ref, rows), BF16),
            vmem((n_ref, 128), F32),
            vmem((nw, 2, 128), F32), vmem((n_ptcl, 2, 128), F32),
            vmem((ny, 2, rows), F32),
            vmem((nw, 128), F32), vmem((n_ptcl, nw, 128), F32),
            vmem((nw, 1, 128), F32), vmem((n_ptcl, 1, 128), F32),
            vmem((nz, nx, 2, LINE, LINE), F32),
            vmem((nz, nx, LINE, LINE), F32),
            vmem((nz, nx - 1, LINE, LINE), BF16), vmem((nz, nx - 1, LINE, LINE), BF16),
            vmem((nz - 1, LINE, LINE), BF16), vmem((nz - 1, LINE, LINE), BF16),
            dma((8,)),
            dma((n_pair,)), dma((n_pair,)), dma((n_pair,)),
            dma((nx,)), dma((nx,)),
            dma(()), dma(()),
            dma((2, 2, nd)), dma((2, 2, nd)),
            dma((2, nd)), dma((2, nd)),
            dma(()), dma(()), dma(()), dma(()), dma(()), dma(()),
            dma((nz,)), dma((nz,)), dma((nz,)), dma((nz,)), dma((nz - 1,)), dma((nz - 1,)),
        ],
        compiler_params=pltpu.CompilerParams(collective_id=0, has_side_effects=True, vmem_limit_bytes=58 << 20),
        cost_estimate=pl.CostEstimate(flops=flops, bytes_accessed=n_ref * pixels * 2, transcendentals=0),
    )(images, bin_lists.T, precision.reshape(1, part), references[0], line_index[0].T, interp_blocks)
    prob, volume = pl.pallas_call(
        hand_on,
        out_shape=(jax.ShapeDtypeStruct((1, part), F32), jax.ShapeDtypeStruct((LINE, LINE), F32)),
        in_specs=[whole, whole],
        out_specs=(whole, whole),
    )(prob, volume)
    return prob.reshape(part, 1), volume[None]


def solution(mesh, nz=NZ):
    in_specs = (
        P("ptcl", None),
        P("ptcl", None),
        P("ptcl"),
        P("cls", "ptcl", None),
        P("cls", "ptcl", None),
        P(),
    )
    out_specs = (P("ptcl", "cls"), P("cls", "ptcl", None))
    return jax.shard_map(functools.partial(local, nz), mesh=mesh, in_specs=in_specs, out_specs=out_specs,
                         check_vma=False)
```

```python
import functools

import jax
import jax.numpy as jnp
from jax import lax
from jax.experimental import pallas as pl
from jax.experimental.pallas import tpu as pltpu
from jax.sharding import PartitionSpec as P

MESH = pl.DeviceIdType.MESH
F32, BF16, I32 = jnp.float32, jnp.bfloat16, jnp.int32
NZ = 8
CW = 128
FAR = 4
HOLD = 1
LAG = 4
AHEAD = 5
LINE = 128
SLOTS = 8


def iota(shape, dim):
    return lax.broadcasted_iota(I32, shape, dim)


def dot(a, b, ca=1, cb=0):
    return lax.dot_general(a, b, (((ca,), (cb,)), ((), ())), preferred_element_type=F32)


def thirds(v):
    hi = v.astype(BF16)
    rest = v - hi.astype(F32)
    mid = rest.astype(BF16)
    low = (rest - mid.astype(F32)).astype(BF16)
    return hi, mid, low


def kernel(ny, nx, nz, nd, far_n, img_hbm, bins_hbm, prec_hbm, refs_hbm, idx_hbm, interp_hbm, prob_ref, vol_ref,
           img, bins_ref, prec_ref, g, g2, sendbuf, recv, xs_all, refs, idx, onehot, interp, score, weight, hnorm,
           psend, ptab, stat, lrow, ltab, dsend, dtab, vb, sib, xs, xr, zs, zr, wr,
           load_sem, a_ss, a_rs, a_loc, h_ss, h_rs, p_ss, p_rs,
           y_ss, y_rs, f_ss, f_rs, s_ss, s_rs, b_ss, b_rs, d_ss, d_rs,
           v_ss, v_rs, x_ss, x_rs, z_ss, z_rs, w_ss, w_rs):
    nq = nx * nz
    y, d = lax.axis_index("cls"), lax.axis_index("ptcl")
    q, k = d // 2, d % 2
    x, z = q // nz, q % nz
    other = 1 - k
    part = bins_ref.shape[1]
    n_bin, pairs = nq * 2, 2 * part
    n_pair = nd + far_n
    n_ref = refs.shape[0]
    rows = n_bin * SLOTS
    nw = rows // 128
    per_w = 128 // SLOTS
    sibling = (y, q * 2 + other)
    y_up, y_dn, y_far = (y + 1) % ny, (y + ny - 1) % ny, (y + 2) % ny
    up, dn = (y_up, d), (y_dn, d)

    def remote(src, dst, ss, rs, dev):
        return pltpu.make_async_remote_copy(src_ref=src, dst_ref=dst, send_sem=ss, recv_sem=rs,
                                            device_id=dev, device_id_type=MESH)

    def piece(yy, h, m):
        return (yy * nd + m) * 2 + h

    def pixels(p, count):
        return pl.ds(pl.multiple_of(p * CW, 2 * CW), count * CW)

    bar = pltpu.get_barrier_semaphore()

    def greet(i, c):
        pl.semaphore_signal(bar, inc=1, device_id=(y, (d + i) % n_bin), device_id_type=MESH)
        return c

    def greet_y(i, c):
        pl.semaphore_signal(bar, inc=1, device_id=((y + i) % ny, d), device_id_type=MESH)
        return c

    lax.fori_loop(1, n_bin, greet, 0)
    lax.fori_loop(1, ny, greet_y, 0)

    loads = [
        pltpu.make_async_copy(img_hbm.at[:, pixels(piece(y, 0, 1), 2 * nd - 2)],
                              img.at[:, pl.ds(2 * CW, (2 * nd - 2) * CW)], load_sem.at[0]),
        pltpu.make_async_copy(img_hbm.at[:, pixels(piece(y_far, 0, nd - far_n), 2 * far_n)],
                              img.at[:, pl.ds(2 * nd * CW, 2 * far_n * CW)], load_sem.at[1]),
        pltpu.make_async_copy(idx_hbm, idx, load_sem.at[2]),
        pltpu.make_async_copy(refs_hbm, refs, load_sem.at[3]),
        pltpu.make_async_copy(interp_hbm, interp, load_sem.at[4]),
    ]
    first = [
        pltpu.make_async_copy(bins_hbm, bins_ref, load_sem.at[5]),
        pltpu.make_async_copy(img_hbm.at[:, pixels(piece(y, 0, 0), 2)], img.at[:, pl.ds(0, 2 * CW)], load_sem.at[6]),
        pltpu.make_async_copy(prec_hbm, prec_ref, load_sem.at[7]),
    ]
    for ld in first + loads:
        ld.start()

    first[0].wait()
    own_bins = bins_ref[...].astype(F32)
    bins = jnp.concatenate([own_bins[0:1], own_bins[1:2]], axis=1)
    before = (iota((pairs, pairs), 0) < iota((pairs, pairs), 1)).astype(F32).astype(BF16)
    named = (iota((n_bin, pairs), 0).astype(F32) == bins).astype(F32)
    rank = named * dot(named.astype(BF16), before)
    expand = (lax.shift_right_logical(iota((rows, n_bin), 0), 3) == iota((rows, n_bin), 1)).astype(F32).astype(BF16)
    spread = dot(expand, (named + rank).astype(BF16))
    hit = (spread == ((iota((rows, pairs), 0) & 7) + 1).astype(F32)).astype(F32)
    g2[...] = hit.astype(BF16)
    g[...] = (hit[:, :part] + hit[:, part:]).astype(BF16)

    def gather(m):
        out = dot(g[...], img[:, 2 * m * CW:2 * (m + 1) * CW])
        halves = [out[:, h * CW:(h + 1) * CW].reshape(n_bin, SLOTS, CW) for h in range(2)]
        sendbuf[:, m] = jnp.concatenate(halves, axis=1).astype(BF16)

    def own_part(m, n, c):
        return pltpu.make_async_copy(sendbuf.at[d, pl.ds(m, n)], recv.at[d, pl.ds(m, n)], a_loc.at[c])

    def send_chunk(m, n, c):
        def send(i, carry):
            d2 = (d + i) % n_bin
            remote(sendbuf.at[d2, pl.ds(m, n)], recv.at[d, pl.ds(m, n)], a_ss.at[c], a_rs.at[c], (y, d2)).start()
            return carry

        lax.fori_loop(1, n_bin, send, 0)
        own_part(m, n, c).start()

    def chunk_all(m, n, c):
        ref = recv.at[pl.ds(0, n_bin - 1), pl.ds(m, n)]
        return remote(ref, ref, a_ss.at[c], a_rs.at[c], sibling)

    group = 2 * nz
    steps_x = sorted(range(nx), key=lambda dx: min(dx, nx - dx))

    def send_head(dx):
        def send(i, carry):
            d2 = ((x + dx) % nx) * group + (d + i) % group
            remote(sendbuf.at[d2, pl.ds(0, 1)], recv.at[d, pl.ds(0, 1)], h_ss.at[dx], h_rs.at[dx], (y, d2)).start()
            return carry

        lax.fori_loop(0 if dx else 1, group, send, 0)

    def head_all(dx):
        ref = recv.at[pl.ds(0, group if dx else group - 1), pl.ds(0, 1)]
        return remote(ref, ref, h_ss.at[dx], h_rs.at[dx], sibling)

    chunks = [(m, 1) for m in range(n_pair)]
    first[1].wait()
    gather(0)
    pl.semaphore_wait(bar, n_bin - 1 + ny - 1)

    def issue(c):
        m, n = chunks[c]
        if c == 1:
            loads[0].wait()
        if c == nd:
            loads[1].wait()
        gather(m)
        send_chunk(m, n, c)

    own_part(0, 1, 0).start()
    for dx in steps_x:
        send_head(dx)
    for c in range(1, min(AHEAD, n_pair)):
        issue(c)

    def own_lanes(t):
        axis = t.ndim - 1
        t = jnp.where(lax.shift_right_logical(iota(t.shape, axis), 3) == d % per_w, t, 0.0)
        for s in (64, 32, 16, 8):
            t = t + pltpu.roll(t, s, axis)
        return t

    def by_device(t):
        t = t.reshape(nw, per_w, t.shape[1], 128)
        return jnp.sum(jnp.where(lax.shift_right_logical(iota(t.shape, 3), 3) == iota(t.shape, 1), t, 0.0), axis=1)

    def in_row(t):
        return jnp.concatenate([t[w:w + 1] for w in range(nw)], axis=1)

    def in_windows(t):
        return jnp.concatenate([t[:, w * 128:(w + 1) * 128] for w in range(nw)], axis=0)

    first[2].wait()
    prec = prec_ref[...].astype(F32)
    ranks = jnp.sum(rank, axis=0, keepdims=True)
    facts = [[prec, prec], [own_bins[1:2], own_bins[0:1]], [ranks[:, part:], ranks[:, :part]]]
    facts = [jnp.concatenate(v, axis=1) for v in facts]
    facts = jnp.concatenate(facts + [jnp.zeros((5, pairs), F32)], axis=0).astype(BF16)
    facts = dot(facts, g2[...], 1, 1)
    facts = jnp.concatenate([facts[0:1], facts[1:2] * SLOTS + facts[2:3]], axis=0)
    for w in range(nw):
        psend[w] = facts[:, w * 128:(w + 1) * 128]

    def send_facts(i, c):
        d2 = (d + i) % n_bin
        remote(psend.at[d2 // per_w], ptab.at[d], p_ss, p_rs, (y, d2)).start()
        return c

    lax.fori_loop(1, n_bin, send_facts, 0)
    ptab[d] = psend[d // per_w]
    facts_done = remote(ptab.at[pl.ds(0, n_bin - 1)], ptab.at[pl.ds(0, n_bin - 1)], p_ss, p_rs, sibling)

    hnorm[...] = jnp.zeros_like(hnorm)
    score[...] = jnp.zeros_like(score)

    def aside(m):
        def norm(i, c):
            v = refs[:, pl.ds(pl.multiple_of(i * 128, 128), 128)].astype(F32)
            hnorm[...] += v * v
            return c

        def bands(i, c):
            onehot[i] = (iota((LINE, n_ref), 0) == idx[pl.ds(i, 1), :]).astype(F32).astype(BF16)
            return c

        count = onehot.shape[0] // nd
        lax.fori_loop(m * count, (m + 1) * count, norm, 0)
        lax.fori_loop(m * count, (m + 1) * count, bands, 0)

    def slab(p):
        return jnp.concatenate([xs_all[p].reshape(rows, CW), xs_all[p + 1].reshape(rows, CW)], axis=1)

    def add_score(p):
        score[...] += dot(refs[:, pixels(p, 2)], slab(p), 1, 1)

    def y_copy(way, h, m):
        ref = xs_all.at[piece(y, h, m)]
        return remote(ref, ref, y_ss.at[way, h, m], y_rs.at[way, h, m], up if way == 0 else dn)

    def f_copy(way, m):
        ref = xs_all.at[piece(y_dn if way == 0 else y_up, way, m)]
        return remote(ref, ref, f_ss.at[way, m], f_rs.at[way, m], up if way == 0 else dn)

    def stage0(c):
        m, n = chunks[c]
        chunk_all(m, n, c).wait_recv()
        own_part(m, n, c).wait()
        for i in range(m, m + n):
            t = recv[:, i].astype(F32)
            for h in range(2):
                p = piece(y, h, i) if i < nd else piece(y_far, h, i - far_n)
                xs_all[p] = t[:, h * SLOTS:(h + 1) * SLOTS].reshape(nq, 16, CW).astype(BF16)
            if i < nd:
                for h in range(2):
                    for way in range(2):
                        y_copy(way, h, i).start()
        if c + AHEAD - 1 < n_pair:
            issue(c + AHEAD - 1)

    def head_copy(way, h, x_src):
        ref = xs_all.at[piece(y, h, 0), pl.ds(x_src * nz, nz)]
        return remote(ref, ref, y_ss.at[way, h, 0], y_rs.at[way, h, 0], up if way == 0 else dn)

    def stage_head():
        own_part(0, 1, 0).wait()
        for dx in steps_x:
            head_all(dx).wait_recv()
            x_src = (x + nx - dx) % nx
            t = recv[pl.ds(x_src * group, group), 0].astype(F32)
            for h in range(2):
                xs_all[piece(y, h, 0), pl.ds(x_src * nz, nz)] = (
                    t[:, h * SLOTS:(h + 1) * SLOTS].reshape(nz, 16, CW).astype(BF16))
                for way in range(2):
                    head_copy(way, h, x_src).start()

    def stage1(m):
        for way in range(2):
            y_copy(way, way, m).wait_recv()
            if m < nd - far_n:
                f_copy(way, m).start()
        add_score(piece(y, 0, m))
        for way in range(2):
            y_copy(way, 1 - way, m).wait_recv()
        add_score(piece(y_dn, 0, m))
        add_score(piece(y_up, 0, m))

    def stage2(m):
        if m < nd - far_n:
            for way in range(2):
                f_copy(way, m).wait_recv()
        add_score(piece(y_far, 0, m))

    loads[2].wait()
    loads[3].wait()
    for m in range(nd):
        if m:
            stage0(m)
        else:
            stage_head()
        if m >= 1:
            stage1(m - 1)
        if 2 <= m < nd - far_n + 2:
            stage2(m - 2)
        aside(m)
    score[...] -= 0.5 * jnp.sum(hnorm[...], axis=1, keepdims=True)
    facts_done.wait_recv()
    known = by_device(own_lanes(ptab[...]))
    scale = in_row(known[:, 0])
    mate = known[:, 1]
    stage1(nd - 1)
    for m in range(nd - 2, nd - far_n):
        stage2(m)
    for c in range(nd, n_pair):
        stage0(c)
        stage2(c - far_n)

    s = scale * score[...]
    score[...] = s
    top = jnp.max(s, axis=0, keepdims=True)
    total = jnp.sum(jnp.exp(s - top), axis=0, keepdims=True)
    stat[y] = jnp.concatenate([top, total], axis=0)

    def share(i, c):
        remote(stat.at[y], stat.at[y], s_ss, s_rs, ((y + i) % ny, d)).start()
        return c

    lax.fori_loop(1, ny, share, 0)
    all_stat = stat.at[pl.ds(0, ny - 1)]
    remote(all_stat, all_stat, s_ss, s_rs, sibling).wait_recv()
    tops = [stat[yy, 0:1] for yy in range(ny)]
    high = functools.reduce(jnp.maximum, tops)
    mine = in_windows(high + jnp.log(sum(stat[yy, 1:2] * jnp.exp(tops[yy] - high) for yy in range(ny))))

    lrow[...] = mine

    def spread_sums(i, c):
        remote(lrow, ltab.at[d], b_ss, b_rs, (y, (d + i) % n_bin)).start()
        return c

    lax.fori_loop(1, n_bin, spread_sums, 0)
    ltab[d] = mine
    all_sums = ltab.at[pl.ds(0, n_bin - 1)]
    remote(all_sums, all_sums, b_ss, b_rs, sibling).wait_recv()
    sums = ltab[...]
    slot = iota((nw, 128), 1) & 7
    key = (iota(sums.shape, 0) * SLOTS + (iota(sums.shape, 2) & 7)).astype(F32)
    theirs = jnp.zeros((nw, 128), F32)
    for delta in range(1 - SLOTS, SLOTS):
        asked = pltpu.roll(mate, delta % 128, 1)
        asked = jnp.where((slot - delta >= 0) & (slot - delta < SLOTS), asked, -1.0)
        found = jnp.sum(jnp.where(key == asked[None], sums, 0.0), axis=0)
        theirs = theirs + pltpu.roll(found, (-delta) % 128, 1)
    high = jnp.maximum(mine, theirs)
    log = in_row(high + jnp.log(jnp.exp(mine - high) + jnp.exp(theirs - high)))
    weight[...] = (n_ref * jnp.exp(score[...] - log)).astype(BF16)

    loads[4].wait()

    def sib_send(t):
        return remote(vb.at[t, :, other], sib.at[t], v_ss.at[t], v_rs.at[t], sibling)

    def x_send(t, i):
        x2 = (x + nx - 1 - i) % nx
        return remote(xs.at[t, i], xr.at[t, i], x_ss.at[t], x_rs.at[t], (y, (x2 * nz + z) * 2 + k))

    def x_all(t, n):
        ref = xr.at[t, pl.ds(0, n)]
        return remote(ref, ref, x_ss.at[t], x_rs.at[t], sibling)

    def is_near(t):
        return (t < 2) | ((t >= nz - 3) & (t < nz - 1))

    def w_send(t):
        z2 = (z + nz - 1 - t) % nz
        return remote(xs.at[t, 1], wr.at[t], w_ss.at[t], w_rs.at[t], (y, (x * nz + z2) * 2 + k))

    def x_wait(t, kind):
        @pl.when(is_near(t))
        def _():
            getattr(x_all(t, nx - 2), kind)()

        @pl.when(jnp.logical_not(is_near(t)))
        def _():
            getattr(x_all(t, nx - 1), kind)()

    def z_send(t):
        z2 = (z + nz - 1 - t) % nz
        return remote(zs.at[t], zr.at[t], z_ss.at[t], z_rs.at[t], (y, (x * nz + z2) * 2 + k))

    def insert(t):
        chips = [((x + nx - 1 - i) % nx) * nz + (z + nz - 1 - t) % nz for i in range(nx)]
        images = [dot(weight[...], slab(2 * c)).astype(BF16) for c in chips]
        sums = [dot(onehot[2 * c + h], im[:, h * LINE:(h + 1) * LINE]) for c, im in zip(chips, images) for h in (0, 1)]
        out = []
        for i in range(nx):
            for h in range(2):
                band = sums[2 * i + h]
                hi = band.astype(BF16)
                low = (band - hi.astype(F32)).astype(BF16)
                block = interp[2 * chips[i] + h]
                out.append(dot(jnp.concatenate([hi, low], axis=1), jnp.concatenate([block, block], axis=0)))
        for i in range(nx):
            for h in range(2):
                vb[t, i, h] = out[2 * i + h]

    def step(t, c):
        @pl.when(t < nz)
        def _():
            insert(t)
            sib_send(t).start()

        @pl.when((t >= HOLD) & (t < nz + HOLD))
        def _():
            u = t - HOLD
            sib_send(u).wait_recv()

            def one(i, c):
                xs[u, i] = (vb[u, i, k] + sib[u, i]).astype(BF16)

                @pl.when((i != 1) | jnp.logical_not(is_near(u) | (u == nz - 1)))
                def _():
                    x_send(u, i).start()

                @pl.when((i == 1) & is_near(u))
                def _():
                    w_send(u).start()

                return c

            lax.fori_loop(0, nx - 1, one, 0)

        @pl.when(t == nz + HOLD)
        def _():
            total = vb[nz - 1, 1, k] + sib[nz - 1, 1]
            for u in (0, 1, nz - 3, nz - 2):
                w_send(u).wait_recv()
                total += wr[u].astype(F32)
            xs[nz - 1, 1] = total.astype(BF16)
            x_send(nz - 1, 1).start()

        @pl.when(t >= LAG)
        def _():
            u = t - LAG
            x_wait(u, "wait_recv")
            total = vb[u, nx - 1, k] + sib[u, nx - 1]
            for i in (0, 2):
                total += xr[u, i].astype(F32)
            total += jnp.where(is_near(u), 0.0, xr[u, 1].astype(F32))

            @pl.when(u < nz - 1)
            def _():
                zs[u] = total.astype(BF16)
                z_send(u).start()

            @pl.when(u == nz - 1)
            def _():
                vol_ref[...] = total

        return c

    lax.fori_loop(0, 2, step, 0)

    chance = stat[y][1:2] * jnp.exp(stat[y][0:1] - log)
    for w in range(nw):
        dsend[w] = chance[:, w * 128:(w + 1) * 128]

    def send_prob(i, c):
        d2 = (d + i) % n_bin
        remote(dsend.at[d2 // per_w], dtab.at[d], d_ss, d_rs, (y, d2)).start()
        return c

    lax.fori_loop(1, n_bin, send_prob, 0)
    dtab[d] = dsend[d // per_w]
    prob_done = remote(dtab.at[pl.ds(0, n_bin - 1)], dtab.at[pl.ds(0, n_bin - 1)], d_ss, d_rs, sibling)

    lax.fori_loop(2, nz + HOLD, step, 0)

    prob_done.wait_recv()
    found = in_row(by_device(own_lanes(dtab[...]))[:, 0])
    found = dot(jnp.concatenate(thirds(found) + (jnp.zeros((5, rows), BF16),), axis=0), g2[...])
    found = (found[2:3] + found[1:2]) + found[0:1]
    prob_ref[...] = found[:, :part] + found[:, part:]

    lax.fori_loop(nz + HOLD, nz + LAG, step, 0)

    def z_add(t, c):
        z_send(t).wait_recv()
        vol_ref[...] += zr[t].astype(F32)
        return c

    lax.fori_loop(0, nz - 1, z_add, 0)

    facts_done.wait_send()
    remote(all_stat, all_stat, s_ss, s_rs, sibling).wait_send()
    remote(all_sums, all_sums, b_ss, b_rs, sibling).wait_send()
    prob_done.wait_send()
    for dx in steps_x:
        head_all(dx).wait_send()
    for c, (m, n) in enumerate(chunks):
        if c:
            chunk_all(m, n, c).wait_send()
    for m in range(nd):
        for way in range(2):
            for h in range(2):
                y_copy(way, h, m).wait_send()
            if m < nd - far_n:
                f_copy(way, m).wait_send()

    def v_done(t, c):
        sib_send(t).wait_send()
        x_wait(t, "wait_send")
        return c

    lax.fori_loop(0, nz, v_done, 0)
    for u in (0, 1, nz - 3, nz - 2):
        w_send(u).wait_send()
    lax.fori_loop(0, nz - 1, lambda t, c: (z_send(t).wait_send(), c)[1], 0)


def hand_on(a_ref, b_ref, c_ref, d_ref):
    c_ref[...] = a_ref[...]
    d_ref[...] = b_ref[...]


def local(nz, images, bin_lists, precision, references, line_index, interp_blocks):
    ny, n_ptcl = lax.axis_size("cls"), lax.axis_size("ptcl")
    nq = n_ptcl // 2
    nx = nq // nz
    part, pixels = images.shape
    n_ref = references.shape[1]
    n_line = interp_blocks.shape[0]
    nd = pixels // (2 * ny * CW)
    n_pair = nd + FAR
    rows = n_ptcl * SLOTS
    nw = rows // 128
    vmem, dma = pltpu.VMEM, pltpu.SemaphoreType.DMA
    whole = pl.BlockSpec(memory_space=pltpu.VMEM)
    far = pl.BlockSpec(memory_space=pl.ANY)
    flops = 4 * n_ref * rows * pixels
    prob, volume = pl.pallas_call(
        functools.partial(kernel, ny, nx, nz, nd, FAR),
        out_shape=(jax.ShapeDtypeStruct((1, part), F32), jax.ShapeDtypeStruct((LINE, LINE), F32)),
        in_specs=[far] * 6,
        out_specs=(whole, whole),
        scratch_shapes=[
            vmem((part, 2 * n_pair * CW), BF16),
            vmem((2, part), I32),
            vmem((1, part), BF16),
            vmem((rows, part), BF16),
            vmem((rows, 2 * part), BF16),
            vmem((n_ptcl, n_pair, 16, CW), BF16),
            vmem((n_ptcl, n_pair, 16, CW), BF16),
            vmem((2 * ny * nd, nq, 16, CW), BF16),
            vmem((n_ref, pixels), BF16),
            vmem((n_line, n_ref), I32),
            vmem((n_line, LINE, n_ref), BF16),
            vmem((n_line, LINE, LINE), BF16),
            vmem((n_ref, rows), F32),
            vmem((n_ref, rows), BF16),
            vmem((n_ref, 128), F32),
            vmem((nw, 2, 128), F32), vmem((n_ptcl, 2, 128), F32),
            vmem((ny, 2, rows), F32),
            vmem((nw, 128), F32), vmem((n_ptcl, nw, 128), F32),
            vmem((nw, 1, 128), F32), vmem((n_ptcl, 1, 128), F32),
            vmem((nz, nx, 2, LINE, LINE), F32),
            vmem((nz, nx, LINE, LINE), F32),
            vmem((nz, nx - 1, LINE, LINE), BF16), vmem((nz, nx - 1, LINE, LINE), BF16),
            vmem((nz - 1, LINE, LINE), BF16), vmem((nz - 1, LINE, LINE), BF16),
            vmem((nz, LINE, LINE), BF16),
            dma((8,)),
            dma((n_pair,)), dma((n_pair,)), dma((n_pair,)),
            dma((nx,)), dma((nx,)),
            dma(()), dma(()),
            dma((2, 2, nd)), dma((2, 2, nd)),
            dma((2, nd)), dma((2, nd)),
            dma(()), dma(()), dma(()), dma(()), dma(()), dma(()),
            dma((nz,)), dma((nz,)), dma((nz,)), dma((nz,)), dma((nz - 1,)), dma((nz - 1,)), dma((nz,)), dma((nz,)),
        ],
        compiler_params=pltpu.CompilerParams(collective_id=0, has_side_effects=True, vmem_limit_bytes=58 << 20),
        cost_estimate=pl.CostEstimate(flops=flops, bytes_accessed=n_ref * pixels * 2, transcendentals=0),
    )(images, bin_lists.T, precision.reshape(1, part), references[0], line_index[0].T, interp_blocks)
    prob, volume = pl.pallas_call(
        hand_on,
        out_shape=(jax.ShapeDtypeStruct((1, part), F32), jax.ShapeDtypeStruct((LINE, LINE), F32)),
        in_specs=[whole, whole],
        out_specs=(whole, whole),
    )(prob, volume)
    return prob.reshape(part, 1), volume[None]


def solution(mesh, nz=NZ):
    in_specs = (
        P("ptcl", None),
        P("ptcl", None),
        P("ptcl"),
        P("cls", "ptcl", None),
        P("cls", "ptcl", None),
        P(),
    )
    out_specs = (P("ptcl", "cls"), P("cls", "ptcl", None))
    return jax.shard_map(functools.partial(local, nz), mesh=mesh, in_specs=in_specs, out_specs=out_specs,
                         check_vma=False)
```
